512 devices in a mesh: dom: 512 (over y, x, z, core).
Axes of the slice: x: 4, y: 8, z: 8, core: 2. Of those that a mesh axis runs over, the one named last changes fastest.
Arguments:
- current: float32 [86528, 768], P('dom'), may hold values from -6 to 6
- previous: float32 [86528, 768], P('dom'), may hold values from -6 to 6
- material: bfloat16 [4608, 25, 768], P('dom'), may hold values from 0.5 to 2
- stepping: float32 [86528], P('dom'), may hold values from 0.01 to 0.1
- point_order: int32 [512, 169], P('dom'), may hold values from 0 to 168, each once within a row
- order_bucket: int32 [512, 9], P('dom'), may hold values from 0 to 3
Outputs:
- following: float32 [86528, 768], P('dom')
The draws below stay inside these ranges and needn't reach their ends.
All inputs are finite; a program needn't handle non-finite values.
Results may differ from the reference program's by a relative error of at most 0.0003.
Values sent between devices are 32-bit elements; how exact they have to be, the bound alone decides.
A program may use at most 64 MiB of HBM per device.

```python
import math
import jax
import jax.numpy as jnp
import numpy as np
from jax import lax

ELEM_SIDE = 3
TIME_STEPS = 2
GRID_COLUMNS = 8
POINT_SIDE = 13
PATCH_POINTS = 169
PATCH_ELEMS = 9
COEF_COLS = 768
PATCH_COUNT = 512


def draw_order_bucket(key, part):
    key = jax.random.fold_in(key, 7)
    level_key, spread_key = jax.random.split(key)
    level = jax.random.randint(level_key, (PATCH_COUNT, 1), 0, 4)
    spread = jax.random.randint(spread_key, (PATCH_COUNT, PATCH_ELEMS), -1, 2)
    return jnp.clip(level + spread, 0, 3).astype(jnp.int32)


def steps_of(stream_key, dims, cuts, least, top_value):
    level = 1.0
    for axis_at, blocks in cuts:
        heights = jax.random.uniform(jax.random.fold_in(jax.random.fold_in(stream_key, 6), axis_at), (blocks,), jnp.float32, least / len(cuts), top_value / len(cuts))
        level = level * jnp.repeat(jnp.exp(heights), dims[axis_at] // blocks).reshape((-1,) + (1,) * (len(dims) - 1 - axis_at))
    return level


def centred(own_key, dims, deviation, reach, shards=(), kind=jnp.bfloat16):
    values = jax.random.normal(own_key, dims, jnp.float32) * deviation
    if len(shards) > 0:
        values = steps_of(own_key, dims, shards, -0.22, 0.18) * values
    return jnp.clip(values, min=-reach, max=reach).astype(kind)


def setup_inputs(seed: int = 0) -> dict:
    key_list = jax.random.split(jax.random.key(seed), 7)
    current = centred(key_list[0], (PATCH_COUNT * PATCH_POINTS, COEF_COLS), 1.0, 6.0, ((0, 512),), jnp.float32)
    previous = centred(key_list[1], (PATCH_COUNT * PATCH_POINTS, COEF_COLS), 1.0, 6.0, ((0, 512),), jnp.float32)
    material = jnp.clip(jnp.exp(math.log(2.0) - 1.3862944 * jax.random.uniform(key_list[2], (PATCH_COUNT * PATCH_ELEMS, 25, COEF_COLS), jnp.float32) ** steps_of(key_list[2], (PATCH_COUNT * PATCH_ELEMS, 25, COEF_COLS), ((0, 512),), -0.2, 0.2)), 0.5, 2.0).astype(jnp.bfloat16)
    stepping = jnp.clip(jnp.exp(math.log(0.1) - 2.3025851 * jax.random.uniform(key_list[3], (PATCH_COUNT * PATCH_POINTS,), jnp.float32) ** steps_of(key_list[3], (PATCH_COUNT * PATCH_POINTS,), ((0, 512),), -0.2, 0.2)), 0.01, 0.1)
    point_order = jax.vmap(lambda own: jax.random.permutation(own, PATCH_POINTS))(jax.random.split(key_list[4], PATCH_COUNT)).reshape((PATCH_COUNT, PATCH_POINTS)).astype(jnp.int32)
    order_bucket = draw_order_bucket(jax.random.fold_in(key_list[6], 71), 0)
    return dict(current=current, previous=previous, material=material, stepping=stepping, point_order=point_order, order_bucket=order_bucket)


TOP_PRECISION = lax.Precision.HIGHEST

def gll_tables():
    gll_nodes = np.array([-1.0, -np.sqrt(3.0 / 7.0), 0.0, np.sqrt(3.0 / 7.0), 1.0])
    weights = np.array([0.1, 49.0 / 90.0, 32.0 / 45.0, 49.0 / 90.0, 0.1])
    barycentric = np.array([1.0 / np.prod([gll_nodes[j] - gll_nodes[k] for k in range(5) if k != j]) for j in range(5)])
    derivative = np.zeros((5, 5))
    for i in range(5):
        for j in range(5):
            if i != j:
                derivative[i, j] = barycentric[j] / barycentric[i] / (gll_nodes[i] - gll_nodes[j])
        derivative[i, i] = -np.sum(derivative[i])
    return (jnp.asarray(derivative, dtype=jnp.float32), jnp.asarray(np.outer(weights, weights), dtype=jnp.float32))

def fourier_tables(coef_cols):
    column = jnp.arange(coef_cols, dtype=jnp.int32)
    wave_order = column // 2
    sample = jnp.arange(coef_cols, dtype=jnp.int32)
    turn_count = wave_order[:, None] * sample[None, :] % coef_cols
    phase_angle = turn_count.astype(jnp.float32) * (2.0 * math.pi / coef_cols)
    inverse = jnp.where((column % 2 == 0)[:, None], jnp.cos(phase_angle), jnp.sin(phase_angle))
    factor = jnp.where(wave_order == 0, 1.0, 2.0).astype(jnp.float32) / coef_cols
    forward = (inverse * factor[:, None]).T
    return (inverse, forward)

def element_points(per_side):
    point_side = 4 * per_side + 1
    positions = np.arange(per_side)
    inside = np.arange(5)
    grid_first = 4 * positions[:, None, None, None] + inside[None, None, :, None]
    grid_second = 4 * positions[None, :, None, None] + inside[None, None, None, :]
    return (grid_first * point_side + grid_second).reshape(per_side * per_side, 25).astype(np.int32)

def order_mask(bucket_row, coef_cols):
    order_limit = jnp.right_shift(jnp.full(bucket_row.shape, coef_cols, jnp.int32), (3 - bucket_row).astype(jnp.int32))
    return jnp.arange(coef_cols, dtype=jnp.int32)[None, :] < order_limit[:, None]

def element_forces(element_rows, material, derivative, quadrature, inverse, forward):
    elem_total = element_rows.shape[0]
    samples = jnp.dot(element_rows.reshape(elem_total * 25, -1), inverse, precision=TOP_PRECISION)
    samples = samples.reshape(elem_total, 5, 5, -1)
    slope_first = jnp.einsum('ac,ecbm->eabm', derivative, samples, precision=TOP_PRECISION)
    slope_second = jnp.einsum('bc,eacm->eabm', derivative, samples, precision=TOP_PRECISION)
    scaled = material.astype(jnp.float32).reshape(elem_total, 5, 5, -1) * quadrature[None, :, :, None]
    stress_first = scaled * slope_first
    stress_second = scaled * slope_second
    element_force = jnp.einsum('ca,ecbm->eabm', derivative, stress_first, precision=TOP_PRECISION)
    element_force = element_force + jnp.einsum('cb,eacm->eabm', derivative, stress_second, precision=TOP_PRECISION)
    result = jnp.dot(element_force.reshape(elem_total * 25, -1), forward, precision=TOP_PRECISION)
    return result.reshape(elem_total, 25, -1)

def reference(current, previous, material, stepping, point_order, order_bucket):
    derivative, quadrature = gll_tables()
    inverse, forward = fourier_tables(COEF_COLS)
    struct_index = jnp.asarray(element_points(ELEM_SIDE))
    material_blocks = material.reshape(PATCH_COUNT, PATCH_ELEMS, 25, COEF_COLS)
    grid_rows = PATCH_COUNT // GRID_COLUMNS
    edge_span = 4 * ELEM_SIDE
    patch_index = jnp.arange(PATCH_COUNT, dtype=jnp.int32)
    base_first = patch_index % GRID_COLUMNS * edge_span
    base_second = patch_index // GRID_COLUMNS * edge_span
    local_index = jnp.arange(PATCH_POINTS, dtype=jnp.int32)
    global_first = base_first[:, None] + (local_index // POINT_SIDE)[None, :]
    global_second = base_second[:, None] + (local_index % POINT_SIDE)[None, :]
    second_extent = grid_rows * edge_span + 1
    flat_global = (global_first * second_extent + global_second).astype(jnp.int32)
    total_points = (GRID_COLUMNS * edge_span + 1) * second_extent

    def one_patch(inputs):
        block, order_row, bucket_row, patch_material = inputs
        struct_field = block[order_row]
        mask_rows = order_mask(bucket_row, COEF_COLS)[:, None, :]
        element_rows = jnp.where(mask_rows, struct_field[struct_index], 0.0)
        coefs = element_forces(element_rows, patch_material, derivative, quadrature, inverse, forward)
        coefs = jnp.where(mask_rows, coefs, 0.0)
        return jax.ops.segment_sum(coefs.reshape(-1, COEF_COLS), struct_index.reshape(-1), num_segments=PATCH_POINTS)

    def assembled(field_now):
        blocks = field_now.reshape(PATCH_COUNT, PATCH_POINTS, COEF_COLS)
        local_force = lax.map(one_patch, (blocks, point_order, order_bucket, material_blocks))
        whole = jax.ops.segment_sum(local_force.reshape(-1, COEF_COLS), flat_global.reshape(-1), num_segments=total_points)
        struct_total = whole[flat_global]
        stored = jnp.zeros_like(struct_total).at[patch_index[:, None], point_order].set(struct_total)
        return stored.reshape(-1, COEF_COLS)
    field_now = current
    field_old = previous
    for step in range(TIME_STEPS):
        field_new = 2.0 * field_now - field_old - stepping[:, None] * assembled(field_now)
        field_old = field_now
        field_now = field_new
    return field_now
```

```python
import functools

import jax
import jax.numpy as jnp
import ml_dtypes
import numpy as np
from jax import lax
from jax.experimental import pallas as pl
from jax.experimental.pallas import tpu as pltpu
from jax.sharding import PartitionSpec as P

ELEM_SIDE = 3
TIME_STEPS = 2
GRID_COLUMNS = 8
SIDE = 4 * ELEM_SIDE + 1
POINTS = SIDE * SIDE
COLS = 768
ELEMS = ELEM_SIDE * ELEM_SIDE
CENTRE = ELEMS // 2
MAIN = 200
ROWS = 240
STORED = 176
HALO = 64

VMEM_GRANT = 48 * 1024 * 1024

MESH = pl.DeviceIdType.MESH
BF16 = jnp.bfloat16
F32 = jnp.float32

ROUTES = (
    (0, 1, 39, 26, 13),
    (0, -1, 26, 39, 13),
    (1, 0, 13, 0, 13),
    (-1, 0, 0, 13, 13),
    (1, 1, 25, 52, 1),
    (-1, 1, 12, 53, 1),
    (1, -1, 13, 54, 1),
    (-1, -1, 0, 55, 1),
)
EDGE_ROWS = 80


def split_np(table):
    high = table.astype(np.float32).astype(ml_dtypes.bfloat16)
    low = (table - high.astype(np.float64)).astype(np.float32).astype(ml_dtypes.bfloat16)
    return np.stack([high, low])


def gll_tables():
    nodes = np.array([-1.0, -np.sqrt(3.0 / 7.0), 0.0, np.sqrt(3.0 / 7.0), 1.0])
    weights = np.array([0.1, 49.0 / 90.0, 32.0 / 45.0, 49.0 / 90.0, 0.1])
    bary = np.array([1.0 / np.prod([nodes[j] - nodes[k] for k in range(5) if k != j]) for j in range(5)])
    derivative = np.zeros((5, 5))
    for i in range(5):
        for j in range(5):
            if i != j:
                derivative[i, j] = bary[j] / bary[i] / (nodes[i] - nodes[j])
        derivative[i, i] = -np.sum(derivative[i])
    return derivative, np.outer(weights, weights)


SHAPES = ((ROWS, STORED), (STORED, 2 * HALO), (EDGE_ROWS, STORED), (EDGE_ROWS, 2 * HALO), (64, 96), (32, 192), (HALO, 2 * EDGE_ROWS))
PACKED = tuple((sum(r for r, _ in SHAPES[:i]), rows, columns) for i, (rows, columns) in enumerate(SHAPES))
PACKED_ROWS = sum(r for r, _ in SHAPES)

DERIV, QUAD = gll_tables()
ODD = [[float(DERIV[i, j] - DERIV[i, 4 - j]) / 2 for j in range(2)] for i in range(2)]
EVEN = [[float(DERIV[i, j] + DERIV[i, 4 - j]) / 2 for j in range(2)] for i in range(2)]
MIDDLE = [float(DERIV[2, j]) for j in range(2)]
ODD_T = [[float(DERIV[c, a] - DERIV[4 - c, a]) / 2 for c in range(2)] for a in range(2)]
EVEN_T = [[float(DERIV[c, a] + DERIV[4 - c, a]) / 2 for c in range(2)] + [float(DERIV[2, a])] for a in range(2)]
MIDDLE_T = [float(DERIV[c, 2]) for c in range(2)]


BLOCKS = ((0, 0), (1, 0), (0, 1), (0, 2), (1, 1), (1, 2))


def block_columns(parity, kind):
    lane = np.arange(128)
    half = (lane % 4) // 2
    source = lane + 2 * (parity - half)
    return 128 * ((kind - (source // 2) % 3) % 3 + 3 * half) + source


def stacked(table):
    high, low = split_np(table)
    return np.concatenate([high, high, low])


def squared(table):
    high, low = split_np(table)
    return np.concatenate([np.concatenate([high, low], axis=1), np.concatenate([high, 0 * low], axis=1)])


def transform_tables():
    sample = np.arange(128)

    def parts(parity, kind):
        column = block_columns(parity, kind)
        order = column // 2
        angle = (order[:, None] * sample[None, :] % COLS) * (2.0 * np.pi / COLS)
        even = (column % 2 == 0)[:, None]
        real = np.where(even, np.cos(angle), np.sin(angle))
        turned = np.where(even, -np.sin(angle), np.cos(angle)) * (np.sqrt(3.0) / 2.0)
        scale = np.where(order == 0, 1.0, 2.0) / COLS
        return real, turned, scale[:, None]

    tables = [[], [], [], []]
    for parity in range(2):
        real, _, scale = parts(parity, 0)
        tables[0].append(squared(real))
        tables[2].append(squared((real * scale).T))
        real1, turned1, scale1 = parts(parity, 1)
        real2, turned2, scale2 = parts(parity, 2)
        real, scale = np.concatenate([real1, real2]), np.concatenate([scale1, scale2])
        both = np.concatenate([real, np.concatenate([turned1, -turned2])], axis=1)
        tables[1].append(stacked(both))
        tables[3].append(stacked((both * scale).T))
    return np.concatenate(tables[0] + tables[1]), np.concatenate(tables[2] + tables[3])


def row_places():
    elem, point = np.full(ROWS, -1), np.full(ROWS, 0)
    outer = [e for e in range(ELEMS) if e != CENTRE]
    elem[:MAIN] = np.tile(outer, 25)
    point[:MAIN] = np.repeat(np.arange(25), 8)
    elem[MAIN : MAIN + 25] = CENTRE
    point[MAIN : MAIN + 25] = np.arange(25)
    return elem, point


def static_tables():
    elem, point = row_places()
    a, b = point // 5, point % 5
    used = elem >= 0
    struct = np.where(used, (4 * (elem // ELEM_SIDE) + a) * SIDE + 4 * (elem % ELEM_SIDE) + b, -1)
    gather = (np.arange(POINTS)[:, None] == struct[None, :]).astype(np.float64)
    gather = np.concatenate([gather, np.zeros((STORED - POINTS, ROWS))])
    place = np.zeros((STORED, HALO))
    along = np.arange(SIDE)
    edges = (along, 12 * SIDE + along, along * SIDE, along * SIDE + 12)
    corners = (0, 12 * SIDE, 12, 12 * SIDE + 12)
    for slot, (edge, corner) in enumerate(zip(edges, corners)):
        place[edge, SIDE * slot + along] = 1.0
        place[corner, 4 * SIDE + slot] = 1.0

    five = np.arange(25)
    fa, fb = five // 5, five % 5
    first = np.where(fb[:, None] == fb[None, :], DERIV[fa[:, None], fa[None, :]], 0.0)
    second = np.where(fa[:, None] == fa[None, :], DERIV[fb[:, None], fb[None, :]], 0.0)
    slope = np.zeros((64, 32))
    slope[:25, :25] = first
    slope[32:57, :25] = second
    weight = np.zeros(64)
    weight[:25] = weight[32:57] = QUAD[fa, fb]

    def across(table):
        high, low = split_np(table)
        return np.concatenate([high, low, high], axis=1)

    rim = np.full(EDGE_ROWS, -1)
    outer = [e for e in range(ELEMS) if e != CENTRE]
    for i in range(5):
        for q, e in enumerate(outer):
            ex, ey = e // ELEM_SIDE, e % ELEM_SIDE
            if ex != 1:
                rim[8 * i + q] = (4 * ex + 2 * ex) * SIDE + 4 * ey + i
            covered = (ex == 0 and i == 0) or (ex == 2 and i == 4)
            if ey != 1 and not covered:
                rim[40 + 8 * i + q] = (4 * ex + i) * SIDE + 6 * ey
    outgoing = np.zeros((HALO, EDGE_ROWS))
    for slot, edge in enumerate(edges):
        outgoing[SIDE * slot : SIDE * slot + SIDE] = edge[:, None] == rim[None, :]
    rim_gather = (rim[:, None] == np.arange(STORED)[None, :]).astype(np.float64)

    twice = lambda table: np.concatenate([table, table], axis=1)
    packed = np.zeros((PACKED_ROWS, 256), ml_dtypes.bfloat16)
    for (first, rows, columns), table in zip(
        PACKED,
        (
            gather.T,
            twice(place),
            rim_gather,
            twice(rim_gather @ place),
            across(slope),
            across(slope.T * weight[None, :]),
            twice(outgoing),
        ),
    ):
        packed[first : first + rows, :columns] = table.astype(ml_dtypes.bfloat16)
    return packed, twice(gather).astype(ml_dtypes.bfloat16)


def split(value):
    high = value.astype(BF16)
    return high, (value - high.astype(F32)).astype(BF16)


def dot(left, right):
    return jnp.dot(left, right, preferred_element_type=F32)


def slope_line(u):
    odd0, odd1, twice = u[0] - u[4], u[1] - u[3], u[2] + u[2]
    even0, even1 = u[0] + u[4] - twice, u[1] + u[3] - twice
    plus, minus = [], []
    for i in range(2):
        plus.append(ODD[i][0] * odd0 + ODD[i][1] * odd1)
        minus.append(EVEN[i][0] * even0 + EVEN[i][1] * even1)
    middle = MIDDLE[0] * odd0 + MIDDLE[1] * odd1
    return [plus[0] + minus[0], plus[1] + minus[1], middle, plus[1] - minus[1], plus[0] - minus[0]]


def force_line(s):
    odd0, odd1 = s[0] - s[4], s[1] - s[3]
    even0, even1 = s[0] + s[4], s[1] + s[3]
    plus, minus = [], []
    for a in range(2):
        plus.append(ODD_T[a][0] * odd0 + ODD_T[a][1] * odd1)
        minus.append(EVEN_T[a][0] * even0 + EVEN_T[a][1] * even1 + EVEN_T[a][2] * s[2])
    middle = MIDDLE_T[0] * odd0 + MIDDLE_T[1] * odd1
    return [plus[0] + minus[0], plus[1] + minus[1], middle, plus[1] - minus[1], plus[0] - minus[0]]


def by_class(value, lane):
    kind_of_lane, early = lax.rem(lane // 2, 3), lax.rem(lane, 4) < 2
    slabs = [value[:, 128 * v : 128 * v + 128] for v in range(6)]
    blocks = {}
    for kind in range(3):
        first, second = [
            jnp.where(
                kind_of_lane == 0,
                slabs[kind + 3 * h],
                jnp.where(kind_of_lane == 1, slabs[(kind - 1) % 3 + 3 * h], slabs[(kind - 2) % 3 + 3 * h]),
            )
            for h in range(2)
        ]
        blocks[0, kind] = jnp.where(early, first, pltpu.roll(second, 2, 1))
        blocks[1, kind] = jnp.where(early, pltpu.roll(first, 126, 1), second)
    return jnp.concatenate([blocks[block] for block in BLOCKS], axis=1)


def by_column(value, lane):
    kind_of_lane, early = lax.rem(lane // 2, 3), lax.rem(lane, 4) < 2
    blocks = {block: value[:, 128 * i : 128 * i + 128] for i, block in enumerate(BLOCKS)}
    halves = [[], []]
    for kind in range(3):
        even, odd = blocks[0, kind], blocks[1, kind]
        halves[0].append(jnp.where(early, even, pltpu.roll(odd, 2, 1)))
        halves[1].append(jnp.where(early, pltpu.roll(even, 126, 1), odd))
    slabs = []
    for v in range(6):
        parts = halves[v // 3]
        slabs.append(
            jnp.where(
                kind_of_lane == 0, parts[v % 3], jnp.where(kind_of_lane == 1, parts[(v + 1) % 3], parts[(v + 2) % 3])
            )
        )
    return jnp.concatenate(slabs, axis=1)


def class_sums(high, low, table):
    first, others = [], []
    for parity in range(2):
        lanes = slice(128 * parity, 128 * parity + 128)
        both = dot(
            jnp.concatenate([high[:, lanes], low[:, lanes]], axis=1), table[256 * parity : 256 * parity + 256, :]
        )
        first.append(both[:, 0:128] + both[:, 128:256])
    for parity in range(2):
        lanes = slice(256 + 256 * parity, 512 + 256 * parity)
        others.append(
            dot(
                jnp.concatenate([high[:, lanes], low[:, lanes], high[:, lanes]], axis=1),
                table[512 + 768 * parity : 1280 + 768 * parity, :],
            )
        )
    return first, others


def sample_blocks(bases, boths):
    parities = []
    for base, both in zip(bases, boths):
        real, turned = both[:, 0:128], both[:, 128:256]
        half = base - 0.5 * real
        parities.append((base + real, half + turned, half - turned))
    out = [None] * 6
    for t in range(3):
        out[2 * t] = parities[0][t] + parities[1][t]
        out[(2 * t + 3) % 6] = parities[0][t] - parities[1][t]
    return out


def coefficients(forces, table):
    out0, out12 = [], []
    for sign in (1, -1):
        parts = []
        for t in range(3):
            one, other = forces[2 * t], forces[(2 * t + 3) % 6]
            parts.append(one + other if sign > 0 else one - other)
        pair = parts[1] + parts[2]
        out0.append(parts[0] + pair)
        out12 += [parts[0] - 0.5 * pair, parts[1] - parts[2]]
    first, others = class_sums(*split(jnp.concatenate(out0 + out12, axis=1)), table)
    return jnp.concatenate(first + others, axis=1)


def rim_tiles(forces, c, picks):
    tiles = []
    for low, high, step, span in ((picks[0], picks[1], 1, 20), (picks[2], picks[3], 5, 4)):
        for i in range(5):
            p = step * i
            one, other = forces[c, 8 * p : 8 * p + 8, :], forces[c, 8 * (p + span) : 8 * (p + span) + 8, :]
            tiles.append(jnp.where(low, one, jnp.where(high, other, 0.0)))
    return jnp.concatenate(tiles, axis=0)


def slope_line(u):
    odd0, odd1, twice = u[0] - u[4], u[1] - u[3], u[2] + u[2]
    even0, even1 = u[0] + u[4] - twice, u[1] + u[3] - twice
    plus, minus = [], []
    for i in range(2):
        plus.append(ODD[i][0] * odd0 + ODD[i][1] * odd1)
        minus.append(EVEN[i][0] * even0 + EVEN[i][1] * even1)
    middle = MIDDLE[0] * odd0 + MIDDLE[1] * odd1
    return [plus[0] + minus[0], plus[1] + minus[1], middle, plus[1] - minus[1], plus[0] - minus[0]]


def force_line(s):
    odd0, odd1 = s[0] - s[4], s[1] - s[3]
    even0, even1 = s[0] + s[4], s[1] + s[3]
    plus, minus = [], []
    for a in range(2):
        plus.append(ODD_T[a][0] * odd0 + ODD_T[a][1] * odd1)
        minus.append(EVEN_T[a][0] * even0 + EVEN_T[a][1] * even1 + EVEN_T[a][2] * s[2])
    middle = MIDDLE_T[0] * odd0 + MIDDLE_T[1] * odd1
    return [plus[0] + minus[0], plus[1] + minus[1], middle, plus[1] - minus[1], plus[0] - minus[0]]


def by_class(value, lane):
    kind_of_lane, early = lax.rem(lane // 2, 3), lax.rem(lane, 4) < 2
    slabs = [value[:, 128 * v : 128 * v + 128] for v in range(6)]
    blocks = {}
    for kind in range(3):
        first, second = [
            jnp.where(
                kind_of_lane == 0,
                slabs[kind + 3 * h],
                jnp.where(kind_of_lane == 1, slabs[(kind - 1) % 3 + 3 * h], slabs[(kind - 2) % 3 + 3 * h]),
            )
            for h in range(2)
        ]
        blocks[0, kind] = jnp.where(early, first, pltpu.roll(second, 2, 1))
        blocks[1, kind] = jnp.where(early, pltpu.roll(first, 126, 1), second)
    return jnp.concatenate([blocks[block] for block in BLOCKS], axis=1)


def by_column(value, lane):
    kind_of_lane, early = lax.rem(lane // 2, 3), lax.rem(lane, 4) < 2
    blocks = {block: value[:, 128 * i : 128 * i + 128] for i, block in enumerate(BLOCKS)}
    halves = [[], []]
    for kind in range(3):
        even, odd = blocks[0, kind], blocks[1, kind]
        halves[0].append(jnp.where(early, even, pltpu.roll(odd, 2, 1)))
        halves[1].append(jnp.where(early, pltpu.roll(even, 126, 1), odd))
    slabs = []
    for v in range(6):
        parts = halves[v // 3]
        slabs.append(
            jnp.where(
                kind_of_lane == 0, parts[v % 3], jnp.where(kind_of_lane == 1, parts[(v + 1) % 3], parts[(v + 2) % 3])
            )
        )
    return jnp.concatenate(slabs, axis=1)


def class_sums(high, low, table):
    first, others = [], []
    for parity in range(2):
        lanes = slice(128 * parity, 128 * parity + 128)
        both = dot(
            jnp.concatenate([high[:, lanes], low[:, lanes]], axis=1), table[256 * parity : 256 * parity + 256, :]
        )
        first.append(both[:, 0:128] + both[:, 128:256])
    for parity in range(2):
        lanes = slice(256 + 256 * parity, 512 + 256 * parity)
        others.append(
            dot(
                jnp.concatenate([high[:, lanes], low[:, lanes], high[:, lanes]], axis=1),
                table[512 + 768 * parity : 1280 + 768 * parity, :],
            )
        )
    return first, others


def sample_blocks(bases, boths):
    parities = []
    for base, both in zip(bases, boths):
        real, turned = both[:, 0:128], both[:, 128:256]
        half = base - 0.5 * real
        parities.append((base + real, half + turned, half - turned))
    out = [None] * 6
    for t in range(3):
        out[2 * t] = parities[0][t] + parities[1][t]
        out[(2 * t + 3) % 6] = parities[0][t] - parities[1][t]
    return out


def force_sums(forces):
    out0, out12 = [], []
    for sign in (1, -1):
        parts = []
        for t in range(3):
            one, other = forces[2 * t, :, :], forces[(2 * t + 3) % 6, :, :]
            parts.append(one + other if sign > 0 else one - other)
        pair = parts[1] + parts[2]
        out0.append(parts[0] + pair)
        out12.append(jnp.concatenate([parts[0] - 0.5 * pair, parts[1] - parts[2]], axis=1))
    return jnp.concatenate(out0, axis=1), jnp.concatenate(out12, axis=1)


def outer_forces(samples, modulus, forces):
    def one_block(c, carry):
        u = [samples[c, 8 * p : 8 * p + 8, :] for p in range(25)]
        total = [None] * 25
        for b in range(5):
            places = [5 * a + b for a in range(5)]
            slopes = slope_line([u[p] for p in places])
            stress = [slopes[a] * modulus[c, 8 * p : 8 * p + 8, :] for a, p in enumerate(places)]
            for p, part in zip(places, force_line(stress)):
                total[p] = part
        for a in range(5):
            places = [5 * a + b for b in range(5)]
            slopes = slope_line([u[p] for p in places])
            stress = [slopes[b] * modulus[c, 8 * p : 8 * p + 8, :] for b, p in enumerate(places)]
            for p, part in zip(places, force_line(stress)):
                forces[c, 8 * p : 8 * p + 8, :] = total[p] + part
        return carry

    lax.fori_loop(0, 6, one_block, 0)


def padded(ref):
    first = lax.broadcasted_iota(jnp.int32, (8, COLS), 0) == 0
    return jnp.concatenate([ref[0:168, :], jnp.where(first, ref[168:169, :], 0.0)], axis=0)


def slabs_of(ref, first, count):
    return jnp.concatenate([ref[c, first : first + count, :] for c in range(6)], axis=1)


def kernel(rows_total, *refs):
    sources, out_ref, held, refs = refs[:10], refs[10], refs[11:21], refs[21:]
    (order_pad, step_pad, mat, mat_centre, samples, forces, keep, field, partial) = refs[:9]
    (scales, collect_ref, assemble, settle, send, recv, load_sem, send_sem, recv_sem) = refs[9:]
    cur, order, packed, bucket, inverse, mat_in, forward, stepping, gather, prev = held

    me = lax.axis_index("dom")
    column = lax.rem(me, GRID_COLUMNS)
    row = lax.div(me, GRID_COLUMNS)

    loads = [pltpu.make_async_copy(sources[i], held[i], load_sem.at[i]) for i in range(10)]
    for load in loads:
        load.start()

    recv[...] = jnp.zeros_like(recv)

    def exists(dc, dr):
        c, r = column + dc, row + dr
        return (c >= 0) & (c < GRID_COLUMNS) & (r >= 0) & (r < rows_total)

    barrier = pltpu.get_barrier_semaphore()
    expected = jnp.int32(0)
    for dc, dr, _, _, _ in ROUTES:
        here = exists(dc, dr)
        expected = expected + here.astype(jnp.int32)

        @pl.when(here)
        def _():
            pl.semaphore_signal(barrier, inc=1, device_id=(me + dc + GRID_COLUMNS * dr,), device_id_type=MESH)

    order_pad[...] = jnp.full(order_pad.shape, -1, jnp.int32)
    step_pad[...] = jnp.zeros_like(step_pad)
    forces[:, MAIN + 32 : ROWS, :] = jnp.zeros((6, ROWS - MAIN - 32, 128), F32)
    mat_centre[...] = jnp.zeros_like(mat_centre)
    lane = lax.broadcasted_iota(jnp.int32, (1, 128), 1)
    q = lax.broadcasted_iota(jnp.int32, (8, 128), 0)
    picks = (q < 3, q >= 5, (q == 0) | (q == 3) | (q == 5), (q == 2) | (q == 4) | (q == 7))

    place_at = lax.broadcasted_iota(jnp.int32, (1, COLS), 1)
    block, inside = place_at >> 7, place_at & 127
    parity = ((block == 1) | (block >= 4)).astype(jnp.int32)
    kind = jnp.where(block < 2, 0, jnp.where((block == 2) | (block == 4), 1, 2))
    half = (inside >> 1) & 1
    source = inside + 2 * (parity - half)
    natural = (128 * (lax.rem(kind + 3 - lax.rem(source >> 1, 3), 3) + 3 * half) + source).astype(F32)

    def table(i):
        first, rows, columns = PACKED[i]
        return packed[first : first + rows, 0:columns]

    loads[1].wait()
    order_pad[0:1, 0:POINTS] = order[...]
    stored_row = lax.broadcasted_iota(jnp.int32, (STORED, STORED), 0)
    one_hot = jnp.where(stored_row == order_pad[0:1, :], 1.0, 0.0).astype(BF16)

    def stored_of(selection):
        return lax.dot_general(selection, one_hot, (((1,), (1,)), ((), ())), preferred_element_type=F32)

    loads[2].wait()
    collect = stored_of(table(0)).astype(BF16)

    loads[3].wait()
    limit_row = lax.shift_right_logical(jnp.full((1, ELEMS), COLS, jnp.int32), 3 - bucket[...]).astype(F32)
    elem_row = lax.broadcasted_iota(jnp.int32, (ROWS, ELEMS), 0)
    inner = lax.rem(elem_row, 8)
    owner = jnp.where(elem_row < MAIN, inner + (inner >= CENTRE).astype(jnp.int32), CENTRE)
    owned = owner == lax.broadcasted_iota(jnp.int32, (ROWS, ELEMS), 1)
    limit_col = jnp.sum(jnp.where(owned, limit_row, 0.0), axis=1, keepdims=True)
    keep[...] = jnp.where(natural < limit_col, 1.0, 0.0).astype(BF16)

    collect_ref[...] = collect
    loads[0].wait()
    field[...] = by_class(padded(cur), lane)
    partial[...] = field[...]

    def exchange(step):
        return [
            (
                pltpu.make_async_remote_copy(
                    src_ref=send.at[step, pl.ds(source, rows)],
                    dst_ref=recv.at[step, pl.ds(target, rows)],
                    send_sem=send_sem.at[step, d],
                    recv_sem=recv_sem.at[step, d],
                    device_id=(me + dc + GRID_COLUMNS * dr,),
                    device_id_type=MESH,
                ),
                exists(dc, dr),
                exists(-dc, -dr),
            )
            for d, (dc, dr, source, target, rows) in enumerate(ROUTES)
        ]

    def arrived(step):
        for copy, _, comes in exchange(step):
            pl.when(comes)(copy.wait_recv)
        return recv[step].reshape(HALO, COLS)

    def one_step(step, carry):
        high, low = [dot(collect_ref[...], half).astype(BF16) * keep[...] for half in split(partial[...])]

        @pl.when(step == 0)
        def _():
            loads[4].wait()

        for c, value in enumerate(sample_blocks(*class_sums(high, low, inverse))):
            samples[c, :, :] = value

        @pl.when(step == 0)
        def _():
            loads[5].wait()
            for e in range(ELEMS):
                if e == CENTRE:
                    mat_centre[0:25, :] = mat_in[e].astype(F32)
                else:
                    for c in range(6):
                        values = mat_in[e, :, 128 * c : 128 * c + 128].astype(F32)
                        mat[c, pl.ds(e - (e > CENTRE), 25, stride=8), :] = values
            for p in range(25):
                mat[:, 8 * p : 8 * p + 8, :] = mat[:, 8 * p : 8 * p + 8, :] * float(QUAD[p // 5, p % 5])
            loads[6].wait()

        @pl.when(step > 0)
        def _():
            rim = dot(table(3), jnp.concatenate(split(arrived(0)), axis=0))
            rim = jnp.where(natural < limit_col[0:EDGE_ROWS], -scales[STORED : STORED + EDGE_ROWS, 0:1] * rim, 0.0)
            for c, value in enumerate(sample_blocks(*class_sums(*split(rim), inverse))):
                for i in range(5):
                    for at, ends in (
                        (8 * i, ((i, picks[0]), (20 + i, picks[1]))),
                        (40 + 8 * i, ((5 * i, picks[2]), (5 * i + 4, picks[3]))),
                    ):
                        tile = value[at : at + 8, :]
                        for p, chosen in ends:
                            samples[c, 8 * p : 8 * p + 8, :] = samples[c, 8 * p : 8 * p + 8, :] + jnp.where(
                                chosen, tile, 0.0
                            )

        outer_forces(samples, mat, forces)
        value = coefficients([rim_tiles(forces, c, picks) for c in range(6)], forward)
        value = jnp.where(natural < limit_col[0:EDGE_ROWS], value, 0.0)
        edges = dot(table(6), jnp.concatenate(split(value), axis=0))
        send[step] = edges.reshape(HALO, 1, COLS)

        @pl.when(step == 0)
        def _():
            pl.semaphore_wait(barrier, expected)

        for copy, goes, _ in exchange(step):
            pl.when(goes)(copy.start)

        high, low = split(slabs_of(samples, MAIN, 32))
        slopes = dot(table(4), jnp.concatenate([high, high, low], axis=0))
        modulus = mat_centre[...]
        high, low = split(jnp.concatenate([slopes[:32] * modulus, slopes[32:] * modulus], axis=0))
        centre = dot(table(5), jnp.concatenate([high, high, low], axis=0))
        for c in range(6):
            forces[c, MAIN : MAIN + 32, :] = centre[:, 128 * c : 128 * c + 128]
        value = coefficients([forces[c, :, :] for c in range(6)], forward)
        coefs = jnp.concatenate(split(jnp.where(natural < limit_col, value, 0.0)), axis=0)

        @pl.when(step == 0)
        def _():
            for load in loads[7:]:
                load.wait()
            step_pad[0:1, 0:POINTS] = stepping[...]
            step_row = step_pad[0:1, :]
            diagonal = stored_row == lax.broadcasted_iota(jnp.int32, (STORED, STORED), 1)
            step_col = jnp.sum(jnp.where(diagonal, step_row, 0.0), axis=1, keepdims=True)
            scales[0:STORED, :] = jnp.broadcast_to(step_col, (STORED, 128))
            rim_step = jnp.sum(stored_of(table(2)) * step_row, axis=1, keepdims=True)
            scales[STORED:, :] = jnp.broadcast_to(rim_step, (EDGE_ROWS, 128))
            assemble[...] = dot(one_hot, gather[...]).astype(BF16)
            settle[...] = dot(one_hot, table(1)).astype(BF16)
            partial[...] = 2.0 * field[...] - by_class(padded(prev), lane)

        @pl.when(step > 0)
        def _():
            settled = dot(settle[...], jnp.concatenate(split(recv[0].reshape(HALO, COLS)), axis=0))
            partial[...] = 2.0 * (partial[...] - scales[0:STORED, 0:1] * settled) - field[...]

        partial[...] = partial[...] - scales[0:STORED, 0:1] * dot(assemble[...], coefs)
        return carry

    lax.fori_loop(0, TIME_STEPS, one_step, 0)
    last = by_column(partial[...], lane)
    settled = dot(settle[...], jnp.concatenate(split(by_column(arrived(TIME_STEPS - 1), lane)), axis=0))
    out_ref[...] = (last - scales[0:STORED, 0:1] * settled)[0:POINTS]
    for step in range(TIME_STEPS):
        for copy, goes, _ in exchange(step):
            pl.when(goes)(copy.wait_send)


def solution(mesh):
    rows_total = mesh.shape["dom"] // GRID_COLUMNS
    inverse, forward = transform_tables()
    packed, gather = static_tables()

    def local(current, previous, material, stepping, point_order, order_bucket):
        operands = [
            current,
            point_order,
            packed,
            order_bucket,
            inverse,
            material,
            forward,
            stepping.reshape(1, POINTS),
            gather,
            previous,
        ]
        operands = [
            pltpu.with_memory_space_constraint(jnp.asarray(operand), pltpu.HBM) for operand in operands
        ]
        return pl.pallas_call(
            functools.partial(kernel, rows_total),
            out_shape=jax.ShapeDtypeStruct((POINTS, COLS), F32),
            in_specs=[pl.BlockSpec(memory_space=pltpu.HBM)] * len(operands),
            out_specs=pl.BlockSpec(memory_space=pltpu.VMEM),
            scratch_shapes=[pltpu.VMEM(operand.shape, operand.dtype) for operand in operands]
            + [
                pltpu.VMEM((8, STORED), jnp.int32),
                pltpu.VMEM((8, STORED), F32),
                pltpu.VMEM((6, MAIN, 128), F32),
                pltpu.VMEM((32, COLS), F32),
                pltpu.VMEM((6, ROWS, 128), F32),
                pltpu.VMEM((6, ROWS, 128), F32),
                pltpu.VMEM((ROWS, COLS), BF16),
                pltpu.VMEM((STORED, COLS), F32),
                pltpu.VMEM((STORED, COLS), F32),
                pltpu.VMEM((STORED + EDGE_ROWS, 128), F32),
                pltpu.VMEM((ROWS, STORED), BF16),
                pltpu.VMEM((STORED, 2 * ROWS), BF16),
                pltpu.VMEM((STORED, 2 * HALO), BF16),
                pltpu.VMEM((TIME_STEPS, HALO, 1, COLS), F32),
                pltpu.VMEM((TIME_STEPS, HALO, 1, COLS), F32),
                pltpu.SemaphoreType.DMA((len(operands),)),
                pltpu.SemaphoreType.DMA((TIME_STEPS, 8)),
                pltpu.SemaphoreType.DMA((TIME_STEPS, 8)),
            ],
            compiler_params=pltpu.CompilerParams(
                collective_id=0, has_side_effects=True, vmem_limit_bytes=VMEM_GRANT
            ),
        )(*operands)

    return jax.shard_map(
        local,
        mesh=mesh,
        in_specs=(
            P("dom", None),
            P("dom", None),
            P("dom", None, None),
            P("dom"),
            P("dom", None),
            P("dom", None),
        ),
        out_specs=P("dom", None),
        check_vma=False,
    )
```

```python
import functools

import jax
import jax.numpy as jnp
import ml_dtypes
import numpy as np
from jax import lax
from jax.experimental import pallas as pl
from jax.experimental.pallas import tpu as pltpu
from jax.sharding import PartitionSpec as P

ELEM_SIDE = 3
TIME_STEPS = 2
GRID_COLUMNS = 8
SIDE = 4 * ELEM_SIDE + 1
POINTS = SIDE * SIDE
COLS = 768
ELEMS = ELEM_SIDE * ELEM_SIDE
CENTRE = ELEMS // 2
MAIN = 200
ROWS = 240
STORED = 176
HALO = 80

VMEM_GRANT = 48 * 1024 * 1024

MESH = pl.DeviceIdType.MESH
BF16 = jnp.bfloat16
F32 = jnp.float32

MESSAGE_ROWS = 384
ROUTES = (
    (1, 1, 344, 320, 8),
    (-1, 1, 336, 328, 8),
    (1, -1, 328, 336, 8),
    (-1, -1, 320, 344, 8),
    (0, 1, 240, 160, 80),
    (0, -1, 160, 240, 80),
    (1, 0, 80, 0, 80),
    (-1, 0, 0, 80, 80),
)
EDGE_ROWS = 80


def split_np(table):
    high = table.astype(np.float32).astype(ml_dtypes.bfloat16)
    low = (table - high.astype(np.float64)).astype(np.float32).astype(ml_dtypes.bfloat16)
    return np.stack([high, low])


def gll_tables():
    nodes = np.array([-1.0, -np.sqrt(3.0 / 7.0), 0.0, np.sqrt(3.0 / 7.0), 1.0])
    weights = np.array([0.1, 49.0 / 90.0, 32.0 / 45.0, 49.0 / 90.0, 0.1])
    bary = np.array([1.0 / np.prod([nodes[j] - nodes[k] for k in range(5) if k != j]) for j in range(5)])
    derivative = np.zeros((5, 5))
    for i in range(5):
        for j in range(5):
            if i != j:
                derivative[i, j] = bary[j] / bary[i] / (nodes[i] - nodes[j])
        derivative[i, i] = -np.sum(derivative[i])
    return derivative, np.outer(weights, weights)


SHAPES = ((ROWS, STORED), (STORED, 2 * HALO), (EDGE_ROWS, STORED), (EDGE_ROWS, 2 * HALO), (64, 96), (32, 192), (HALO, 2 * EDGE_ROWS))
PACKED = tuple((sum(r for r, _ in SHAPES[:i]), rows, columns) for i, (rows, columns) in enumerate(SHAPES))
PACKED_ROWS = sum(r for r, _ in SHAPES)

DERIV, QUAD = gll_tables()
ODD = [[float(DERIV[i, j] - DERIV[i, 4 - j]) / 2 for j in range(2)] for i in range(2)]
EVEN = [[float(DERIV[i, j] + DERIV[i, 4 - j]) / 2 for j in range(2)] for i in range(2)]
MIDDLE = [float(DERIV[2, j]) for j in range(2)]
ODD_T = [[float(DERIV[c, a] - DERIV[4 - c, a]) / 2 for c in range(2)] for a in range(2)]
EVEN_T = [[float(DERIV[c, a] + DERIV[4 - c, a]) / 2 for c in range(2)] + [float(DERIV[2, a])] for a in range(2)]
MIDDLE_T = [float(DERIV[c, 2]) for c in range(2)]


BLOCKS = ((0, 0), (1, 0), (0, 1), (0, 2), (1, 1), (1, 2))


def block_columns(parity, kind):
    lane = np.arange(128)
    half = (lane % 4) // 2
    source = lane + 2 * (parity - half)
    return 128 * ((kind - (source // 2) % 3) % 3 + 3 * half) + source


def stacked(table):
    high, low = split_np(table)
    return np.concatenate([high, high, low])


def squared(table):
    high, low = split_np(table)
    return np.concatenate([np.concatenate([high, low], axis=1), np.concatenate([high, 0 * low], axis=1)])


def transform_tables():
    sample = np.arange(128)

    def parts(parity, kind):
        column = block_columns(parity, kind)
        order = column // 2
        angle = (order[:, None] * sample[None, :] % COLS) * (2.0 * np.pi / COLS)
        even = (column % 2 == 0)[:, None]
        real = np.where(even, np.cos(angle), np.sin(angle))
        turned = np.where(even, -np.sin(angle), np.cos(angle)) * (np.sqrt(3.0) / 2.0)
        scale = np.where(order == 0, 1.0, 2.0) / COLS
        return real, turned, scale[:, None]

    tables = [[], [], [], []]
    for parity in range(2):
        real, _, scale = parts(parity, 0)
        tables[0].append(squared(real))
        tables[2].append(squared((real * scale).T))
        real1, turned1, scale1 = parts(parity, 1)
        real2, turned2, scale2 = parts(parity, 2)
        real, scale = np.concatenate([real1, real2]), np.concatenate([scale1, scale2])
        both = np.concatenate([real, np.concatenate([turned1, -turned2])], axis=1)
        tables[1].append(stacked(both))
        tables[3].append(stacked((both * scale).T))
    return np.concatenate(tables[0] + tables[1]), np.concatenate(tables[2] + tables[3])


def row_places():
    elem, point = np.full(ROWS, -1), np.full(ROWS, 0)
    outer = [e for e in range(ELEMS) if e != CENTRE]
    elem[:MAIN] = np.tile(outer, 25)
    point[:MAIN] = np.repeat(np.arange(25), 8)
    elem[MAIN : MAIN + 25] = CENTRE
    point[MAIN : MAIN + 25] = np.arange(25)
    return elem, point


def static_tables():
    elem, point = row_places()
    a, b = point // 5, point % 5
    used = elem >= 0
    struct = np.where(used, (4 * (elem // ELEM_SIDE) + a) * SIDE + 4 * (elem % ELEM_SIDE) + b, -1)
    gather = (np.arange(POINTS)[:, None] == struct[None, :]).astype(np.float64)
    gather = np.concatenate([gather, np.zeros((STORED - POINTS, ROWS))])
    place = np.zeros((STORED, HALO))
    along = np.arange(SIDE)
    edges = (along, 12 * SIDE + along, along * SIDE, along * SIDE + 12)
    corners = (0, 12 * SIDE, 12, 12 * SIDE + 12)
    for slot, (edge, corner) in enumerate(zip(edges, corners)):
        place[edge, 16 * slot + along] = 1.0
        place[corner, 64 + slot] = 1.0

    five = np.arange(25)
    fa, fb = five // 5, five % 5
    first = np.where(fb[:, None] == fb[None, :], DERIV[fa[:, None], fa[None, :]], 0.0)
    second = np.where(fa[:, None] == fa[None, :], DERIV[fb[:, None], fb[None, :]], 0.0)
    slope = np.zeros((64, 32))
    slope[:25, :25] = first
    slope[32:57, :25] = second
    weight = np.zeros(64)
    weight[:25] = weight[32:57] = QUAD[fa, fb]

    def across(table):
        high, low = split_np(table)
        return np.concatenate([high, low, high], axis=1)

    rim = np.full(EDGE_ROWS, -1)
    outer = [e for e in range(ELEMS) if e != CENTRE]
    for i in range(5):
        for q, e in enumerate(outer):
            ex, ey = e // ELEM_SIDE, e % ELEM_SIDE
            if ex != 1:
                rim[8 * i + q] = (4 * ex + 2 * ex) * SIDE + 4 * ey + i
            covered = (ex == 0 and i == 0) or (ex == 2 and i == 4)
            if ey != 1 and not covered:
                rim[40 + 8 * i + q] = (4 * ex + i) * SIDE + 6 * ey
    outgoing = np.zeros((HALO, EDGE_ROWS))
    for slot, (edge, corner) in enumerate(zip(edges, corners)):
        outgoing[16 * slot : 16 * slot + SIDE] = edge[:, None] == rim[None, :]
        outgoing[64 + slot] = corner == rim
    rim_gather = (rim[:, None] == np.arange(STORED)[None, :]).astype(np.float64)

    twice = lambda table: np.concatenate([table, table], axis=1)
    packed = np.zeros((PACKED_ROWS, 256), ml_dtypes.bfloat16)
    for (first, rows, columns), table in zip(
        PACKED,
        (
            gather.T,
            twice(place),
            rim_gather,
            twice(rim_gather @ place),
            across(slope),
            across(slope.T * weight[None, :]),
            twice(outgoing),
        ),
    ):
        packed[first : first + rows, :columns] = table.astype(ml_dtypes.bfloat16)
    return packed, twice(gather).astype(ml_dtypes.bfloat16)


def split(value):
    high = value.astype(BF16)
    return high, (value - high.astype(F32)).astype(BF16)


def dot(left, right):
    return jnp.dot(left, right, preferred_element_type=F32)


def slope_line(u):
    odd0, odd1, twice = u[0] - u[4], u[1] - u[3], u[2] + u[2]
    even0, even1 = u[0] + u[4] - twice, u[1] + u[3] - twice
    plus, minus = [], []
    for i in range(2):
        plus.append(ODD[i][0] * odd0 + ODD[i][1] * odd1)
        minus.append(EVEN[i][0] * even0 + EVEN[i][1] * even1)
    middle = MIDDLE[0] * odd0 + MIDDLE[1] * odd1
    return [plus[0] + minus[0], plus[1] + minus[1], middle, plus[1] - minus[1], plus[0] - minus[0]]


def force_line(s):
    odd0, odd1 = s[0] - s[4], s[1] - s[3]
    even0, even1 = s[0] + s[4], s[1] + s[3]
    plus, minus = [], []
    for a in range(2):
        plus.append(ODD_T[a][0] * odd0 + ODD_T[a][1] * odd1)
        minus.append(EVEN_T[a][0] * even0 + EVEN_T[a][1] * even1 + EVEN_T[a][2] * s[2])
    middle = MIDDLE_T[0] * odd0 + MIDDLE_T[1] * odd1
    return [plus[0] + minus[0], plus[1] + minus[1], middle, plus[1] - minus[1], plus[0] - minus[0]]


def by_class(value, lane):
    kind_of_lane, early = lax.rem(lane // 2, 3), lax.rem(lane, 4) < 2
    slabs = [value[:, 128 * v : 128 * v + 128] for v in range(6)]
    blocks = {}
    for kind in range(3):
        first, second = [
            jnp.where(
                kind_of_lane == 0,
                slabs[kind + 3 * h],
                jnp.where(kind_of_lane == 1, slabs[(kind - 1) % 3 + 3 * h], slabs[(kind - 2) % 3 + 3 * h]),
            )
            for h in range(2)
        ]
        blocks[0, kind] = jnp.where(early, first, pltpu.roll(second, 2, 1))
        blocks[1, kind] = jnp.where(early, pltpu.roll(first, 126, 1), second)
    return jnp.concatenate([blocks[block] for block in BLOCKS], axis=1)


def by_column(value, lane):
    kind_of_lane, early = lax.rem(lane // 2, 3), lax.rem(lane, 4) < 2
    blocks = {block: value[:, 128 * i : 128 * i + 128] for i, block in enumerate(BLOCKS)}
    halves = [[], []]
    for kind in range(3):
        even, odd = blocks[0, kind], blocks[1, kind]
        halves[0].append(jnp.where(early, even, pltpu.roll(odd, 2, 1)))
        halves[1].append(jnp.where(early, pltpu.roll(even, 126, 1), odd))
    slabs = []
    for v in range(6):
        parts = halves[v // 3]
        slabs.append(
            jnp.where(
                kind_of_lane == 0, parts[v % 3], jnp.where(kind_of_lane == 1, parts[(v + 1) % 3], parts[(v + 2) % 3])
            )
        )
    return jnp.concatenate(slabs, axis=1)


def class_sums(high, low, table):
    first, others = [], []
    for parity in range(2):
        lanes = slice(128 * parity, 128 * parity + 128)
        both = dot(
            jnp.concatenate([high[:, lanes], low[:, lanes]], axis=1), table[256 * parity : 256 * parity + 256, :]
        )
        first.append(both[:, 0:128] + both[:, 128:256])
    for parity in range(2):
        lanes = slice(256 + 256 * parity, 512 + 256 * parity)
        others.append(
            dot(
                jnp.concatenate([high[:, lanes], low[:, lanes], high[:, lanes]], axis=1),
                table[512 + 768 * parity : 1280 + 768 * parity, :],
            )
        )
    return first, others


def sample_blocks(bases, boths):
    parities = []
    for base, both in zip(bases, boths):
        real, turned = both[:, 0:128], both[:, 128:256]
        half = base - 0.5 * real
        parities.append((base + real, half + turned, half - turned))
    out = [None] * 6
    for t in range(3):
        out[2 * t] = parities[0][t] + parities[1][t]
        out[(2 * t + 3) % 6] = parities[0][t] - parities[1][t]
    return out


def coefficients(forces, table):
    out0, out12 = [], []
    for sign in (1, -1):
        parts = []
        for t in range(3):
            one, other = forces[2 * t], forces[(2 * t + 3) % 6]
            parts.append(one + other if sign > 0 else one - other)
        pair = parts[1] + parts[2]
        out0.append(parts[0] + pair)
        out12 += [parts[0] - 0.5 * pair, parts[1] - parts[2]]
    first, others = class_sums(*split(jnp.concatenate(out0 + out12, axis=1)), table)
    return jnp.concatenate(first + others, axis=1)


def rim_tiles(forces, c, picks):
    tiles = []
    for low, high, step, span in ((picks[0], picks[1], 1, 20), (picks[2], picks[3], 5, 4)):
        for i in range(5):
            p = step * i
            one, other = forces[c, 8 * p : 8 * p + 8, :], forces[c, 8 * (p + span) : 8 * (p + span) + 8, :]
            tiles.append(jnp.where(low, one, jnp.where(high, other, 0.0)))
    return jnp.concatenate(tiles, axis=0)


def slope_line(u):
    odd0, odd1, twice = u[0] - u[4], u[1] - u[3], u[2] + u[2]
    even0, even1 = u[0] + u[4] - twice, u[1] + u[3] - twice
    plus, minus = [], []
    for i in range(2):
        plus.append(ODD[i][0] * odd0 + ODD[i][1] * odd1)
        minus.append(EVEN[i][0] * even0 + EVEN[i][1] * even1)
    middle = MIDDLE[0] * odd0 + MIDDLE[1] * odd1
    return [plus[0] + minus[0], plus[1] + minus[1], middle, plus[1] - minus[1], plus[0] - minus[0]]


def force_line(s):
    odd0, odd1 = s[0] - s[4], s[1] - s[3]
    even0, even1 = s[0] + s[4], s[1] + s[3]
    plus, minus = [], []
    for a in range(2):
        plus.append(ODD_T[a][0] * odd0 + ODD_T[a][1] * odd1)
        minus.append(EVEN_T[a][0] * even0 + EVEN_T[a][1] * even1 + EVEN_T[a][2] * s[2])
    middle = MIDDLE_T[0] * odd0 + MIDDLE_T[1] * odd1
    return [plus[0] + minus[0], plus[1] + minus[1], middle, plus[1] - minus[1], plus[0] - minus[0]]


def by_class(value, lane):
    kind_of_lane, early = lax.rem(lane // 2, 3), lax.rem(lane, 4) < 2
    slabs = [value[:, 128 * v : 128 * v + 128] for v in range(6)]
    blocks = {}
    for kind in range(3):
        first, second = [
            jnp.where(
                kind_of_lane == 0,
                slabs[kind + 3 * h],
                jnp.where(kind_of_lane == 1, slabs[(kind - 1) % 3 + 3 * h], slabs[(kind - 2) % 3 + 3 * h]),
            )
            for h in range(2)
        ]
        blocks[0, kind] = jnp.where(early, first, pltpu.roll(second, 2, 1))
        blocks[1, kind] = jnp.where(early, pltpu.roll(first, 126, 1), second)
    return jnp.concatenate([blocks[block] for block in BLOCKS], axis=1)


def by_column(value, lane):
    kind_of_lane, early = lax.rem(lane // 2, 3), lax.rem(lane, 4) < 2
    blocks = {block: value[:, 128 * i : 128 * i + 128] for i, block in enumerate(BLOCKS)}
    halves = [[], []]
    for kind in range(3):
        even, odd = blocks[0, kind], blocks[1, kind]
        halves[0].append(jnp.where(early, even, pltpu.roll(odd, 2, 1)))
        halves[1].append(jnp.where(early, pltpu.roll(even, 126, 1), odd))
    slabs = []
    for v in range(6):
        parts = halves[v // 3]
        slabs.append(
            jnp.where(
                kind_of_lane == 0, parts[v % 3], jnp.where(kind_of_lane == 1, parts[(v + 1) % 3], parts[(v + 2) % 3])
            )
        )
    return jnp.concatenate(slabs, axis=1)


def class_sums(high, low, table):
    first, others = [], []
    for parity in range(2):
        lanes = slice(128 * parity, 128 * parity + 128)
        both = dot(
            jnp.concatenate([high[:, lanes], low[:, lanes]], axis=1), table[256 * parity : 256 * parity + 256, :]
        )
        first.append(both[:, 0:128] + both[:, 128:256])
    for parity in range(2):
        lanes = slice(256 + 256 * parity, 512 + 256 * parity)
        others.append(
            dot(
                jnp.concatenate([high[:, lanes], low[:, lanes], high[:, lanes]], axis=1),
                table[512 + 768 * parity : 1280 + 768 * parity, :],
            )
        )
    return first, others


def sample_blocks(bases, boths):
    parities = []
    for base, both in zip(bases, boths):
        real, turned = both[:, 0:128], both[:, 128:256]
        half = base - 0.5 * real
        parities.append((base + real, half + turned, half - turned))
    out = [None] * 6
    for t in range(3):
        out[2 * t] = parities[0][t] + parities[1][t]
        out[(2 * t + 3) % 6] = parities[0][t] - parities[1][t]
    return out


def force_sums(forces):
    out0, out12 = [], []
    for sign in (1, -1):
        parts = []
        for t in range(3):
            one, other = forces[2 * t, :, :], forces[(2 * t + 3) % 6, :, :]
            parts.append(one + other if sign > 0 else one - other)
        pair = parts[1] + parts[2]
        out0.append(parts[0] + pair)
        out12.append(jnp.concatenate([parts[0] - 0.5 * pair, parts[1] - parts[2]], axis=1))
    return jnp.concatenate(out0, axis=1), jnp.concatenate(out12, axis=1)


def outer_forces(samples, modulus, forces):
    def one_block(c, carry):
        u = [samples[c, 8 * p : 8 * p + 8, :] for p in range(25)]
        total = [None] * 25
        for b in range(5):
            places = [5 * a + b for a in range(5)]
            slopes = slope_line([u[p] for p in places])
            stress = [slopes[a] * modulus[c, 8 * p : 8 * p + 8, :] for a, p in enumerate(places)]
            for p, part in zip(places, force_line(stress)):
                total[p] = part
        for a in range(5):
            places = [5 * a + b for b in range(5)]
            slopes = slope_line([u[p] for p in places])
            stress = [slopes[b] * modulus[c, 8 * p : 8 * p + 8, :] for b, p in enumerate(places)]
            for p, part in zip(places, force_line(stress)):
                forces[c, 8 * p : 8 * p + 8, :] = total[p] + part
        return carry

    lax.fori_loop(0, 6, one_block, 0)


def padded(ref):
    first = lax.broadcasted_iota(jnp.int32, (8, COLS), 0) == 0
    return jnp.concatenate([ref[0:168, :], jnp.where(first, ref[168:169, :], 0.0)], axis=0)


def slabs_of(ref, first, count):
    return jnp.concatenate([ref[c, first : first + count, :] for c in range(6)], axis=1)


def kernel(rows_total, *refs):
    sources, out_ref, held, refs = refs[:10], refs[10], refs[11:21], refs[21:]
    (order_pad, step_pad, mat, mat_centre, samples, forces, keep, field, partial) = refs[:9]
    (scales, collect_ref, assemble, settle, send, recv, load_sem, send_sem, recv_sem) = refs[9:]
    cur, order, packed, bucket, inverse, mat_in, forward, stepping, gather, prev = held

    me = lax.axis_index("dom")
    column = lax.rem(me, GRID_COLUMNS)
    row = lax.div(me, GRID_COLUMNS)

    loads = [pltpu.make_async_copy(sources[i], held[i], load_sem.at[i]) for i in range(10)]
    for i in (1, 2, 0, 3, 5, 4):
        loads[i].start()

    recv[...] = jnp.zeros_like(recv)
    for e in range(4):
        send[:, 80 * e + 72 : 80 * e + 80, :] = jnp.zeros((TIME_STEPS, 8, 128), F32)
    send[:, 320:352, :] = jnp.zeros((TIME_STEPS, 32, 128), F32)

    def exists(dc, dr):
        c, r = column + dc, row + dr
        return (c >= 0) & (c < GRID_COLUMNS) & (r >= 0) & (r < rows_total)

    barrier = pltpu.get_barrier_semaphore()
    expected = jnp.int32(0)
    for dc, dr, _, _, _ in ROUTES:
        here = exists(dc, dr)
        expected = expected + here.astype(jnp.int32)

        @pl.when(here)
        def _():
            pl.semaphore_signal(barrier, inc=1, device_id=(me + dc + GRID_COLUMNS * dr,), device_id_type=MESH)

    order_pad[...] = jnp.full(order_pad.shape, -1, jnp.int32)
    step_pad[...] = jnp.zeros_like(step_pad)
    forces[:, MAIN + 32 : ROWS, :] = jnp.zeros((6, ROWS - MAIN - 32, 128), F32)
    mat_centre[...] = jnp.zeros_like(mat_centre)
    lane = lax.broadcasted_iota(jnp.int32, (1, 128), 1)
    q = lax.broadcasted_iota(jnp.int32, (8, 128), 0)
    picks = (q < 3, q >= 5, (q == 0) | (q == 3) | (q == 5), (q == 2) | (q == 4) | (q == 7))

    place_at = lax.broadcasted_iota(jnp.int32, (1, COLS), 1)
    block, inside = place_at >> 7, place_at & 127
    parity = ((block == 1) | (block >= 4)).astype(jnp.int32)
    kind = jnp.where(block < 2, 0, jnp.where((block == 2) | (block == 4), 1, 2))
    half = (inside >> 1) & 1
    source = inside + 2 * (parity - half)
    natural = (128 * (lax.rem(kind + 3 - lax.rem(source >> 1, 3), 3) + 3 * half) + source).astype(F32)

    def table(i):
        first, rows, columns = PACKED[i]
        return packed[first : first + rows, 0:columns]

    loads[1].wait()
    order_pad[0:1, 0:POINTS] = order[...]
    stored_row = lax.broadcasted_iota(jnp.int32, (STORED, STORED), 0)
    one_hot = jnp.where(stored_row == order_pad[0:1, :], 1.0, 0.0).astype(BF16)

    def stored_of(selection):
        return lax.dot_general(selection, one_hot, (((1,), (1,)), ((), ())), preferred_element_type=F32)

    loads[2].wait()
    collect = stored_of(table(0)).astype(BF16)

    loads[3].wait()
    limit_row = lax.shift_right_logical(jnp.full((1, ELEMS), COLS, jnp.int32), 3 - bucket[...]).astype(F32)
    elem_row = lax.broadcasted_iota(jnp.int32, (ROWS, ELEMS), 0)
    inner = lax.rem(elem_row, 8)
    owner = jnp.where(elem_row < MAIN, inner + (inner >= CENTRE).astype(jnp.int32), CENTRE)
    owned = owner == lax.broadcasted_iota(jnp.int32, (ROWS, ELEMS), 1)
    limit_col = jnp.sum(jnp.where(owned, limit_row, 0.0), axis=1, keepdims=True)
    keep[...] = jnp.where(natural < limit_col, 1.0, 0.0).astype(BF16)

    collect_ref[...] = collect
    loads[0].wait()
    field[...] = by_class(padded(cur), lane)
    partial[...] = field[...]
    for load in loads[6:]:
        load.start()
    loads[5].wait()
    for e in range(ELEMS):
        if e == CENTRE:
            mat_centre[0:25, :] = mat_in[e].astype(F32)
        else:
            for c in range(6):
                values = mat_in[e, :, 128 * c : 128 * c + 128].astype(F32)
                mat[c, pl.ds(e - (e > CENTRE), 25, stride=8), :] = values
    for p in range(25):
        mat[:, 8 * p : 8 * p + 8, :] = mat[:, 8 * p : 8 * p + 8, :] * float(QUAD[p // 5, p % 5])

    def exchange(step):
        return [
            (
                pltpu.make_async_remote_copy(
                    src_ref=send.at[step, pl.ds(source, rows)],
                    dst_ref=recv.at[step, pl.ds(target, rows)],
                    send_sem=send_sem.at[step, d],
                    recv_sem=recv_sem.at[step, d],
                    device_id=(me + dc + GRID_COLUMNS * dr,),
                    device_id_type=MESH,
                ),
                exists(dc, dr),
                exists(-dc, -dr),
            )
            for d, (dc, dr, source, target, rows) in enumerate(ROUTES)
        ]

    def halo_rows(step):
        columns = []
        for c in range(6):
            tiles = [recv[step, pl.ds(80 * e + c, 16, stride=6), :] for e in range(4)]
            tiles += [recv[step, pl.ds(320 + c, 8, stride=8), :], jnp.zeros((8, 128), F32)]
            columns.append(jnp.concatenate(tiles, axis=0))
        return jnp.concatenate(columns, axis=1)

    def arrived(step):
        for copy, _, comes in exchange(step):
            pl.when(comes)(copy.wait_recv)
        return halo_rows(step)

    def one_step(step, carry):
        high, low = [dot(collect_ref[...], half).astype(BF16) * keep[...] for half in split(partial[...])]

        @pl.when(step == 0)
        def _():
            loads[4].wait()

        for c, value in enumerate(sample_blocks(*class_sums(high, low, inverse))):
            samples[c, :, :] = value

        @pl.when(step == 0)
        def _():
            loads[6].wait()

        @pl.when(step > 0)
        def _():
            rim = dot(table(3), jnp.concatenate(split(arrived(0)), axis=0))
            rim = jnp.where(natural < limit_col[0:EDGE_ROWS], -scales[STORED : STORED + EDGE_ROWS, 0:1] * rim, 0.0)
            for c, value in enumerate(sample_blocks(*class_sums(*split(rim), inverse))):
                for i in range(5):
                    for at, ends in (
                        (8 * i, ((i, picks[0]), (20 + i, picks[1]))),
                        (40 + 8 * i, ((5 * i, picks[2]), (5 * i + 4, picks[3]))),
                    ):
                        tile = value[at : at + 8, :]
                        for p, chosen in ends:
                            samples[c, 8 * p : 8 * p + 8, :] = samples[c, 8 * p : 8 * p + 8, :] + jnp.where(
                                chosen, tile, 0.0
                            )

        outer_forces(samples, mat, forces)
        value = coefficients([rim_tiles(forces, c, picks) for c in range(6)], forward)
        value = jnp.where(natural < limit_col[0:EDGE_ROWS], value, 0.0)
        edges = dot(table(6), jnp.concatenate(split(value), axis=0))
        for c in range(6):
            values = edges[:, 128 * c : 128 * c + 128]
            for e in range(4):
                send[step, pl.ds(80 * e + c, SIDE, stride=6), :] = values[16 * e : 16 * e + SIDE]
            send[step, pl.ds(320 + c, 4, stride=8), :] = values[64:68]

        @pl.when(step == 0)
        def _():
            pl.semaphore_wait(barrier, expected)

        for copy, goes, _ in exchange(step):
            pl.when(goes)(copy.start)

        high, low = split(slabs_of(samples, MAIN, 32))
        slopes = dot(table(4), jnp.concatenate([high, high, low], axis=0))
        modulus = mat_centre[...]
        high, low = split(jnp.concatenate([slopes[:32] * modulus, slopes[32:] * modulus], axis=0))
        centre = dot(table(5), jnp.concatenate([high, high, low], axis=0))
        for c in range(6):
            forces[c, MAIN : MAIN + 32, :] = centre[:, 128 * c : 128 * c + 128]
        value = coefficients([forces[c, :, :] for c in range(6)], forward)
        coefs = jnp.concatenate(split(jnp.where(natural < limit_col, value, 0.0)), axis=0)

        @pl.when(step == 0)
        def _():
            for load in loads[7:]:
                load.wait()
            step_pad[0:1, 0:POINTS] = stepping[...]
            step_row = step_pad[0:1, :]
            diagonal = stored_row == lax.broadcasted_iota(jnp.int32, (STORED, STORED), 1)
            step_col = jnp.sum(jnp.where(diagonal, step_row, 0.0), axis=1, keepdims=True)
            scales[0:STORED, :] = jnp.broadcast_to(step_col, (STORED, 128))
            rim_step = jnp.sum(stored_of(table(2)) * step_row, axis=1, keepdims=True)
            scales[STORED:, :] = jnp.broadcast_to(rim_step, (EDGE_ROWS, 128))
            assemble[...] = dot(one_hot, gather[...]).astype(BF16)
            settle[...] = dot(one_hot, table(1)).astype(BF16)
            partial[...] = 2.0 * field[...] - by_class(padded(prev), lane)

        @pl.when(step > 0)
        def _():
            settled = dot(settle[...], jnp.concatenate(split(halo_rows(0)), axis=0))
            partial[...] = 2.0 * (partial[...] - scales[0:STORED, 0:1] * settled) - field[...]

        partial[...] = partial[...] - scales[0:STORED, 0:1] * dot(assemble[...], coefs)
        return carry

    lax.fori_loop(0, TIME_STEPS, one_step, 0)
    last = by_column(partial[...], lane)
    settled = dot(settle[...], jnp.concatenate(split(by_column(arrived(TIME_STEPS - 1), lane)), axis=0))
    out_ref[...] = (last - scales[0:STORED, 0:1] * settled)[0:POINTS]
    for step in range(TIME_STEPS):
        for copy, goes, _ in exchange(step):
            pl.when(goes)(copy.wait_send)


def solution(mesh):
    rows_total = mesh.shape["dom"] // GRID_COLUMNS
    inverse, forward = transform_tables()
    packed, gather = static_tables()

    def local(current, previous, material, stepping, point_order, order_bucket):
        operands = [
            current,
            point_order,
            packed,
            order_bucket,
            inverse,
            material,
            forward,
            stepping.reshape(1, POINTS),
            gather,
            previous,
        ]
        operands = [
            pltpu.with_memory_space_constraint(jnp.asarray(operand), pltpu.HBM) for operand in operands
        ]
        return pl.pallas_call(
            functools.partial(kernel, rows_total),
            out_shape=jax.ShapeDtypeStruct((POINTS, COLS), F32),
            in_specs=[pl.BlockSpec(memory_space=pltpu.HBM)] * len(operands),
            out_specs=pl.BlockSpec(memory_space=pltpu.VMEM),
            scratch_shapes=[pltpu.VMEM(operand.shape, operand.dtype) for operand in operands]
            + [
                pltpu.VMEM((8, STORED), jnp.int32),
                pltpu.VMEM((8, STORED), F32),
                pltpu.VMEM((6, MAIN, 128), F32),
                pltpu.VMEM((32, COLS), F32),
                pltpu.VMEM((6, ROWS, 128), F32),
                pltpu.VMEM((6, ROWS, 128), F32),
                pltpu.VMEM((ROWS, COLS), BF16),
                pltpu.VMEM((STORED, COLS), F32),
                pltpu.VMEM((STORED, COLS), F32),
                pltpu.VMEM((STORED + EDGE_ROWS, 128), F32),
                pltpu.VMEM((ROWS, STORED), BF16),
                pltpu.VMEM((STORED, 2 * ROWS), BF16),
                pltpu.VMEM((STORED, 2 * HALO), BF16),
                pltpu.VMEM((TIME_STEPS, MESSAGE_ROWS, 128), F32),
                pltpu.VMEM((TIME_STEPS, MESSAGE_ROWS, 128), F32),
                pltpu.SemaphoreType.DMA((len(operands),)),
                pltpu.SemaphoreType.DMA((TIME_STEPS, 8)),
                pltpu.SemaphoreType.DMA((TIME_STEPS, 8)),
            ],
            compiler_params=pltpu.CompilerParams(
                collective_id=0, has_side_effects=True, vmem_limit_bytes=VMEM_GRANT
            ),
        )(*operands)

    return jax.shard_map(
        local,
        mesh=mesh,
        in_specs=(
            P("dom", None),
            P("dom", None),
            P("dom", None, None),
            P("dom"),
            P("dom", None),
            P("dom", None),
        ),
        out_specs=P("dom", None),
        check_vma=False,
    )
```

```python
import functools

import jax
import jax.numpy as jnp
import ml_dtypes
import numpy as np
from jax import lax
from jax.experimental import pallas as pl
from jax.experimental.pallas import tpu as pltpu
from jax.sharding import PartitionSpec as P

ELEM_SIDE = 3
TIME_STEPS = 2
GRID_COLUMNS = 8
SIDE = 4 * ELEM_SIDE + 1
POINTS = SIDE * SIDE
COLS = 768
ELEMS = ELEM_SIDE * ELEM_SIDE
CENTRE = ELEMS // 2
MAIN = 200
ROWS = 240
STORED = 176
HALO = 80

VMEM_GRANT = 48 * 1024 * 1024

MESH = pl.DeviceIdType.MESH
BF16 = jnp.bfloat16
F32 = jnp.float32

MESSAGE_ROWS = 384
ROUTES = (
    (0, 1, 240, 160, 80),
    (0, -1, 160, 240, 80),
    (1, 1, 344, 320, 8),
    (-1, 1, 336, 328, 8),
    (1, -1, 328, 336, 8),
    (-1, -1, 320, 344, 8),
    (1, 0, 80, 0, 80),
    (-1, 0, 0, 80, 80),
)
EDGE_ROWS = 80


def split_np(table):
    high = table.astype(np.float32).astype(ml_dtypes.bfloat16)
    low = (table - high.astype(np.float64)).astype(np.float32).astype(ml_dtypes.bfloat16)
    return np.stack([high, low])


def gll_tables():
    nodes = np.array([-1.0, -np.sqrt(3.0 / 7.0), 0.0, np.sqrt(3.0 / 7.0), 1.0])
    weights = np.array([0.1, 49.0 / 90.0, 32.0 / 45.0, 49.0 / 90.0, 0.1])
    bary = np.array([1.0 / np.prod([nodes[j] - nodes[k] for k in range(5) if k != j]) for j in range(5)])
    derivative = np.zeros((5, 5))
    for i in range(5):
        for j in range(5):
            if i != j:
                derivative[i, j] = bary[j] / bary[i] / (nodes[i] - nodes[j])
        derivative[i, i] = -np.sum(derivative[i])
    return derivative, np.outer(weights, weights)


SHAPES = ((ROWS, STORED), (STORED, 2 * HALO), (EDGE_ROWS, STORED), (EDGE_ROWS, 2 * HALO), (64, 96), (32, 192), (HALO, 2 * EDGE_ROWS))
PACKED = tuple((sum(r for r, _ in SHAPES[:i]), rows, columns) for i, (rows, columns) in enumerate(SHAPES))
PACKED_ROWS = sum(r for r, _ in SHAPES)

DERIV, QUAD = gll_tables()
ODD = [[float(DERIV[i, j] - DERIV[i, 4 - j]) / 2 for j in range(2)] for i in range(2)]
EVEN = [[float(DERIV[i, j] + DERIV[i, 4 - j]) / 2 for j in range(2)] for i in range(2)]
MIDDLE = [float(DERIV[2, j]) for j in range(2)]
ODD_T = [[float(DERIV[c, a] - DERIV[4 - c, a]) / 2 for c in range(2)] for a in range(2)]
EVEN_T = [[float(DERIV[c, a] + DERIV[4 - c, a]) / 2 for c in range(2)] + [float(DERIV[2, a])] for a in range(2)]
MIDDLE_T = [float(DERIV[c, 2]) for c in range(2)]


BLOCKS = ((0, 0), (1, 0), (0, 1), (0, 2), (1, 1), (1, 2))


def block_columns(parity, kind):
    lane = np.arange(128)
    half = (lane % 4) // 2
    source = lane + 2 * (parity - half)
    return 128 * ((kind - (source // 2) % 3) % 3 + 3 * half) + source


def stacked(table):
    high, low = split_np(table)
    return np.concatenate([high, high, low])


def squared(table):
    high, low = split_np(table)
    return np.concatenate([np.concatenate([high, low], axis=1), np.concatenate([high, 0 * low], axis=1)])


def transform_tables():
    sample = np.arange(128)

    def parts(parity, kind):
        column = block_columns(parity, kind)
        order = column // 2
        angle = (order[:, None] * sample[None, :] % COLS) * (2.0 * np.pi / COLS)
        even = (column % 2 == 0)[:, None]
        real = np.where(even, np.cos(angle), np.sin(angle))
        turned = np.where(even, -np.sin(angle), np.cos(angle)) * (np.sqrt(3.0) / 2.0)
        scale = np.where(order == 0, 1.0, 2.0) / COLS
        return real, turned, scale[:, None]

    tables = [[], [], [], []]
    for parity in range(2):
        real, _, scale = parts(parity, 0)
        tables[0].append(squared(real))
        tables[2].append(squared((real * scale).T))
        real1, turned1, scale1 = parts(parity, 1)
        real2, turned2, scale2 = parts(parity, 2)
        real, scale = np.concatenate([real1, real2]), np.concatenate([scale1, scale2])
        both = np.concatenate([real, np.concatenate([turned1, -turned2])], axis=1)
        tables[1].append(stacked(both))
        tables[3].append(stacked((both * scale).T))
    return np.concatenate(tables[0] + tables[1]), np.concatenate(tables[2] + tables[3])


def row_places():
    elem, point = np.full(ROWS, -1), np.full(ROWS, 0)
    outer = [e for e in range(ELEMS) if e != CENTRE]
    elem[:MAIN] = np.tile(outer, 25)
    point[:MAIN] = np.repeat(np.arange(25), 8)
    elem[MAIN : MAIN + 25] = CENTRE
    point[MAIN : MAIN + 25] = np.arange(25)
    return elem, point


def static_tables():
    elem, point = row_places()
    a, b = point // 5, point % 5
    used = elem >= 0
    struct = np.where(used, (4 * (elem // ELEM_SIDE) + a) * SIDE + 4 * (elem % ELEM_SIDE) + b, -1)
    gather = (np.arange(POINTS)[:, None] == struct[None, :]).astype(np.float64)
    gather = np.concatenate([gather, np.zeros((STORED - POINTS, ROWS))])
    place = np.zeros((STORED, HALO))
    along = np.arange(SIDE)
    edges = (along, 12 * SIDE + along, along * SIDE, along * SIDE + 12)
    corners = (0, 12 * SIDE, 12, 12 * SIDE + 12)
    for slot, (edge, corner) in enumerate(zip(edges, corners)):
        place[edge, 16 * slot + along] = 1.0
        place[corner, 64 + slot] = 1.0

    five = np.arange(25)
    fa, fb = five // 5, five % 5
    first = np.where(fb[:, None] == fb[None, :], DERIV[fa[:, None], fa[None, :]], 0.0)
    second = np.where(fa[:, None] == fa[None, :], DERIV[fb[:, None], fb[None, :]], 0.0)
    slope = np.zeros((64, 32))
    slope[:25, :25] = first
    slope[32:57, :25] = second
    weight = np.zeros(64)
    weight[:25] = weight[32:57] = QUAD[fa, fb]

    def across(table):
        high, low = split_np(table)
        return np.concatenate([high, low, high], axis=1)

    rim = np.full(EDGE_ROWS, -1)
    outer = [e for e in range(ELEMS) if e != CENTRE]
    for i in range(5):
        for q, e in enumerate(outer):
            ex, ey = e // ELEM_SIDE, e % ELEM_SIDE
            if ex != 1:
                rim[8 * i + q] = (4 * ex + 2 * ex) * SIDE + 4 * ey + i
            covered = (ex == 0 and i == 0) or (ex == 2 and i == 4)
            if ey != 1 and not covered:
                rim[40 + 8 * i + q] = (4 * ex + i) * SIDE + 6 * ey
    outgoing = np.zeros((HALO, EDGE_ROWS))
    for slot, (edge, corner) in enumerate(zip(edges, corners)):
        outgoing[16 * slot : 16 * slot + SIDE] = edge[:, None] == rim[None, :]
        outgoing[64 + slot] = corner == rim
    rim_gather = (rim[:, None] == np.arange(STORED)[None, :]).astype(np.float64)

    twice = lambda table: np.concatenate([table, table], axis=1)
    packed = np.zeros((PACKED_ROWS, 256), ml_dtypes.bfloat16)
    for (first, rows, columns), table in zip(
        PACKED,
        (
            gather.T,
            twice(place),
            rim_gather,
            twice(rim_gather @ place),
            across(slope),
            across(slope.T * weight[None, :]),
            twice(outgoing),
        ),
    ):
        packed[first : first + rows, :columns] = table.astype(ml_dtypes.bfloat16)
    return packed, twice(gather).astype(ml_dtypes.bfloat16)


def split(value):
    high = value.astype(BF16)
    return high, (value - high.astype(F32)).astype(BF16)


def dot(left, right):
    return jnp.dot(left, right, preferred_element_type=F32)


def slope_line(u):
    odd0, odd1, twice = u[0] - u[4], u[1] - u[3], u[2] + u[2]
    even0, even1 = u[0] + u[4] - twice, u[1] + u[3] - twice
    plus, minus = [], []
    for i in range(2):
        plus.append(ODD[i][0] * odd0 + ODD[i][1] * odd1)
        minus.append(EVEN[i][0] * even0 + EVEN[i][1] * even1)
    middle = MIDDLE[0] * odd0 + MIDDLE[1] * odd1
    return [plus[0] + minus[0], plus[1] + minus[1], middle, plus[1] - minus[1], plus[0] - minus[0]]


def force_line(s):
    odd0, odd1 = s[0] - s[4], s[1] - s[3]
    even0, even1 = s[0] + s[4], s[1] + s[3]
    plus, minus = [], []
    for a in range(2):
        plus.append(ODD_T[a][0] * odd0 + ODD_T[a][1] * odd1)
        minus.append(EVEN_T[a][0] * even0 + EVEN_T[a][1] * even1 + EVEN_T[a][2] * s[2])
    middle = MIDDLE_T[0] * odd0 + MIDDLE_T[1] * odd1
    return [plus[0] + minus[0], plus[1] + minus[1], middle, plus[1] - minus[1], plus[0] - minus[0]]


def by_class(value, lane):
    kind_of_lane, early = lax.rem(lane // 2, 3), lax.rem(lane, 4) < 2
    slabs = [value[:, 128 * v : 128 * v + 128] for v in range(6)]
    blocks = {}
    for kind in range(3):
        first, second = [
            jnp.where(
                kind_of_lane == 0,
                slabs[kind + 3 * h],
                jnp.where(kind_of_lane == 1, slabs[(kind - 1) % 3 + 3 * h], slabs[(kind - 2) % 3 + 3 * h]),
            )
            for h in range(2)
        ]
        blocks[0, kind] = jnp.where(early, first, pltpu.roll(second, 2, 1))
        blocks[1, kind] = jnp.where(early, pltpu.roll(first, 126, 1), second)
    return jnp.concatenate([blocks[block] for block in BLOCKS], axis=1)


def by_column(value, lane):
    kind_of_lane, early = lax.rem(lane // 2, 3), lax.rem(lane, 4) < 2
    blocks = {block: value[:, 128 * i : 128 * i + 128] for i, block in enumerate(BLOCKS)}
    halves = [[], []]
    for kind in range(3):
        even, odd = blocks[0, kind], blocks[1, kind]
        halves[0].append(jnp.where(early, even, pltpu.roll(odd, 2, 1)))
        halves[1].append(jnp.where(early, pltpu.roll(even, 126, 1), odd))
    slabs = []
    for v in range(6):
        parts = halves[v // 3]
        slabs.append(
            jnp.where(
                kind_of_lane == 0, parts[v % 3], jnp.where(kind_of_lane == 1, parts[(v + 1) % 3], parts[(v + 2) % 3])
            )
        )
    return jnp.concatenate(slabs, axis=1)


def class_sums(high, low, table):
    first, others = [], []
    for parity in range(2):
        lanes = slice(128 * parity, 128 * parity + 128)
        both = dot(
            jnp.concatenate([high[:, lanes], low[:, lanes]], axis=1), table[256 * parity : 256 * parity + 256, :]
        )
        first.append(both[:, 0:128] + both[:, 128:256])
    for parity in range(2):
        lanes = slice(256 + 256 * parity, 512 + 256 * parity)
        others.append(
            dot(
                jnp.concatenate([high[:, lanes], low[:, lanes], high[:, lanes]], axis=1),
                table[512 + 768 * parity : 1280 + 768 * parity, :],
            )
        )
    return first, others


def sample_blocks(bases, boths):
    parities = []
    for base, both in zip(bases, boths):
        real, turned = both[:, 0:128], both[:, 128:256]
        half = base - 0.5 * real
        parities.append((base + real, half + turned, half - turned))
    out = [None] * 6
    for t in range(3):
        out[2 * t] = parities[0][t] + parities[1][t]
        out[(2 * t + 3) % 6] = parities[0][t] - parities[1][t]
    return out


def coefficients(forces, table):
    out0, out12 = [], []
    for sign in (1, -1):
        parts = []
        for t in range(3):
            one, other = forces[2 * t], forces[(2 * t + 3) % 6]
            parts.append(one + other if sign > 0 else one - other)
        pair = parts[1] + parts[2]
        out0.append(parts[0] + pair)
        out12 += [parts[0] - 0.5 * pair, parts[1] - parts[2]]
    first, others = class_sums(*split(jnp.concatenate(out0 + out12, axis=1)), table)
    return jnp.concatenate(first + others, axis=1)


def rim_tiles(forces, c, picks):
    tiles = []
    for low, high, step, span in ((picks[0], picks[1], 1, 20), (picks[2], picks[3], 5, 4)):
        for i in range(5):
            p = step * i
            one, other = forces[c, 8 * p : 8 * p + 8, :], forces[c, 8 * (p + span) : 8 * (p + span) + 8, :]
            tiles.append(jnp.where(low, one, jnp.where(high, other, 0.0)))
    return jnp.concatenate(tiles, axis=0)


def slope_line(u):
    odd0, odd1, twice = u[0] - u[4], u[1] - u[3], u[2] + u[2]
    even0, even1 = u[0] + u[4] - twice, u[1] + u[3] - twice
    plus, minus = [], []
    for i in range(2):
        plus.append(ODD[i][0] * odd0 + ODD[i][1] * odd1)
        minus.append(EVEN[i][0] * even0 + EVEN[i][1] * even1)
    middle = MIDDLE[0] * odd0 + MIDDLE[1] * odd1
    return [plus[0] + minus[0], plus[1] + minus[1], middle, plus[1] - minus[1], plus[0] - minus[0]]


def force_line(s):
    odd0, odd1 = s[0] - s[4], s[1] - s[3]
    even0, even1 = s[0] + s[4], s[1] + s[3]
    plus, minus = [], []
    for a in range(2):
        plus.append(ODD_T[a][0] * odd0 + ODD_T[a][1] * odd1)
        minus.append(EVEN_T[a][0] * even0 + EVEN_T[a][1] * even1 + EVEN_T[a][2] * s[2])
    middle = MIDDLE_T[0] * odd0 + MIDDLE_T[1] * odd1
    return [plus[0] + minus[0], plus[1] + minus[1], middle, plus[1] - minus[1], plus[0] - minus[0]]


def by_class(value, lane):
    kind_of_lane, early = lax.rem(lane // 2, 3), lax.rem(lane, 4) < 2
    slabs = [value[:, 128 * v : 128 * v + 128] for v in range(6)]
    blocks = {}
    for kind in range(3):
        first, second = [
            jnp.where(
                kind_of_lane == 0,
                slabs[kind + 3 * h],
                jnp.where(kind_of_lane == 1, slabs[(kind - 1) % 3 + 3 * h], slabs[(kind - 2) % 3 + 3 * h]),
            )
            for h in range(2)
        ]
        blocks[0, kind] = jnp.where(early, first, pltpu.roll(second, 2, 1))
        blocks[1, kind] = jnp.where(early, pltpu.roll(first, 126, 1), second)
    return jnp.concatenate([blocks[block] for block in BLOCKS], axis=1)


def by_column(value, lane):
    kind_of_lane, early = lax.rem(lane // 2, 3), lax.rem(lane, 4) < 2
    blocks = {block: value[:, 128 * i : 128 * i + 128] for i, block in enumerate(BLOCKS)}
    halves = [[], []]
    for kind in range(3):
        even, odd = blocks[0, kind], blocks[1, kind]
        halves[0].append(jnp.where(early, even, pltpu.roll(odd, 2, 1)))
        halves[1].append(jnp.where(early, pltpu.roll(even, 126, 1), odd))
    slabs = []
    for v in range(6):
        parts = halves[v // 3]
        slabs.append(
            jnp.where(
                kind_of_lane == 0, parts[v % 3], jnp.where(kind_of_lane == 1, parts[(v + 1) % 3], parts[(v + 2) % 3])
            )
        )
    return jnp.concatenate(slabs, axis=1)


def class_sums(high, low, table):
    first, others = [], []
    for parity in range(2):
        lanes = slice(128 * parity, 128 * parity + 128)
        both = dot(
            jnp.concatenate([high[:, lanes], low[:, lanes]], axis=1), table[256 * parity : 256 * parity + 256, :]
        )
        first.append(both[:, 0:128] + both[:, 128:256])
    for parity in range(2):
        lanes = slice(256 + 256 * parity, 512 + 256 * parity)
        others.append(
            dot(
                jnp.concatenate([high[:, lanes], low[:, lanes], high[:, lanes]], axis=1),
                table[512 + 768 * parity : 1280 + 768 * parity, :],
            )
        )
    return first, others


def sample_blocks(bases, boths):
    parities = []
    for base, both in zip(bases, boths):
        real, turned = both[:, 0:128], both[:, 128:256]
        half = base - 0.5 * real
        parities.append((base + real, half + turned, half - turned))
    out = [None] * 6
    for t in range(3):
        out[2 * t] = parities[0][t] + parities[1][t]
        out[(2 * t + 3) % 6] = parities[0][t] - parities[1][t]
    return out


def force_sums(forces):
    out0, out12 = [], []
    for sign in (1, -1):
        parts = []
        for t in range(3):
            one, other = forces[2 * t, :, :], forces[(2 * t + 3) % 6, :, :]
            parts.append(one + other if sign > 0 else one - other)
        pair = parts[1] + parts[2]
        out0.append(parts[0] + pair)
        out12.append(jnp.concatenate([parts[0] - 0.5 * pair, parts[1] - parts[2]], axis=1))
    return jnp.concatenate(out0, axis=1), jnp.concatenate(out12, axis=1)


def outer_forces(samples, modulus, forces):
    def one_block(c, carry):
        u = [samples[c, 8 * p : 8 * p + 8, :] for p in range(25)]
        total = [None] * 25
        for b in range(5):
            places = [5 * a + b for a in range(5)]
            slopes = slope_line([u[p] for p in places])
            stress = [slopes[a] * modulus[c, 8 * p : 8 * p + 8, :] for a, p in enumerate(places)]
            for p, part in zip(places, force_line(stress)):
                total[p] = part
        for a in range(5):
            places = [5 * a + b for b in range(5)]
            slopes = slope_line([u[p] for p in places])
            stress = [slopes[b] * modulus[c, 8 * p : 8 * p + 8, :] for b, p in enumerate(places)]
            for p, part in zip(places, force_line(stress)):
                forces[c, 8 * p : 8 * p + 8, :] = total[p] + part
        return carry

    lax.fori_loop(0, 6, one_block, 0)


def padded(ref):
    first = lax.broadcasted_iota(jnp.int32, (8, COLS), 0) == 0
    return jnp.concatenate([ref[0:168, :], jnp.where(first, ref[168:169, :], 0.0)], axis=0)


def slabs_of(ref, first, count):
    return jnp.concatenate([ref[c, first : first + count, :] for c in range(6)], axis=1)


def kernel(rows_total, *refs):
    sources, out_ref, held, refs = refs[:10], refs[10], refs[11:21], refs[21:]
    (order_pad, step_pad, mat, mat_centre, samples, forces, keep, field, partial) = refs[:9]
    (scales, collect_ref, assemble, settle, send, recv, load_sem, send_sem, recv_sem) = refs[9:]
    cur, order, packed, bucket, inverse, mat_in, forward, stepping, gather, prev = held

    me = lax.axis_index("dom")
    column = lax.rem(me, GRID_COLUMNS)
    row = lax.div(me, GRID_COLUMNS)

    loads = [pltpu.make_async_copy(sources[i], held[i], load_sem.at[i]) for i in range(10)]
    for i in (1, 2, 0, 3, 5, 4):
        loads[i].start()

    recv[...] = jnp.zeros_like(recv)
    for e in range(4):
        send[:, 80 * e + 72 : 80 * e + 80, :] = jnp.zeros((TIME_STEPS, 8, 128), F32)
    send[:, 320:352, :] = jnp.zeros((TIME_STEPS, 32, 128), F32)

    def exists(dc, dr):
        c, r = column + dc, row + dr
        return (c >= 0) & (c < GRID_COLUMNS) & (r >= 0) & (r < rows_total)

    barrier = pltpu.get_barrier_semaphore()
    expected = jnp.int32(0)
    for dc, dr, _, _, _ in ROUTES:
        here = exists(dc, dr)
        expected = expected + here.astype(jnp.int32)

        @pl.when(here)
        def _():
            pl.semaphore_signal(barrier, inc=1, device_id=(me + dc + GRID_COLUMNS * dr,), device_id_type=MESH)

    order_pad[...] = jnp.full(order_pad.shape, -1, jnp.int32)
    step_pad[...] = jnp.zeros_like(step_pad)
    forces[:, MAIN + 32 : ROWS, :] = jnp.zeros((6, ROWS - MAIN - 32, 128), F32)
    mat_centre[...] = jnp.zeros_like(mat_centre)
    lane = lax.broadcasted_iota(jnp.int32, (1, 128), 1)
    q = lax.broadcasted_iota(jnp.int32, (8, 128), 0)
    picks = (q < 3, q >= 5, (q == 0) | (q == 3) | (q == 5), (q == 2) | (q == 4) | (q == 7))

    place_at = lax.broadcasted_iota(jnp.int32, (1, COLS), 1)
    block, inside = place_at >> 7, place_at & 127
    parity = ((block == 1) | (block >= 4)).astype(jnp.int32)
    kind = jnp.where(block < 2, 0, jnp.where((block == 2) | (block == 4), 1, 2))
    half = (inside >> 1) & 1
    source = inside + 2 * (parity - half)
    natural = (128 * (lax.rem(kind + 3 - lax.rem(source >> 1, 3), 3) + 3 * half) + source).astype(F32)

    def table(i):
        first, rows, columns = PACKED[i]
        return packed[first : first + rows, 0:columns]

    loads[1].wait()
    order_pad[0:1, 0:POINTS] = order[...]
    stored_row = lax.broadcasted_iota(jnp.int32, (STORED, STORED), 0)
    one_hot = jnp.where(stored_row == order_pad[0:1, :], 1.0, 0.0).astype(BF16)

    def stored_of(selection):
        return lax.dot_general(selection, one_hot, (((1,), (1,)), ((), ())), preferred_element_type=F32)

    loads[2].wait()
    collect = stored_of(table(0)).astype(BF16)

    loads[3].wait()
    limit_row = lax.shift_right_logical(jnp.full((1, ELEMS), COLS, jnp.int32), 3 - bucket[...]).astype(F32)
    elem_row = lax.broadcasted_iota(jnp.int32, (ROWS, ELEMS), 0)
    inner = lax.rem(elem_row, 8)
    owner = jnp.where(elem_row < MAIN, inner + (inner >= CENTRE).astype(jnp.int32), CENTRE)
    owned = owner == lax.broadcasted_iota(jnp.int32, (ROWS, ELEMS), 1)
    limit_col = jnp.sum(jnp.where(owned, limit_row, 0.0), axis=1, keepdims=True)
    keep[...] = jnp.where(natural < limit_col, 1.0, 0.0).astype(BF16)

    collect_ref[...] = collect
    loads[0].wait()
    field[...] = by_class(padded(cur), lane)
    partial[...] = field[...]
    for load in loads[6:]:
        load.start()
    loads[5].wait()
    for e in range(ELEMS):
        if e == CENTRE:
            mat_centre[0:25, :] = mat_in[e].astype(F32)
        else:
            for c in range(6):
                values = mat_in[e, :, 128 * c : 128 * c + 128].astype(F32)
                mat[c, pl.ds(e - (e > CENTRE), 25, stride=8), :] = values
    for p in range(25):
        mat[:, 8 * p : 8 * p + 8, :] = mat[:, 8 * p : 8 * p + 8, :] * float(QUAD[p // 5, p % 5])

    def exchange(step):
        return [
            (
                pltpu.make_async_remote_copy(
                    src_ref=send.at[step, pl.ds(source, rows)],
                    dst_ref=recv.at[step, pl.ds(target, rows)],
                    send_sem=send_sem.at[step, d],
                    recv_sem=recv_sem.at[step, d],
                    device_id=(me + dc + GRID_COLUMNS * dr,),
                    device_id_type=MESH,
                ),
                exists(dc, dr),
                exists(-dc, -dr),
            )
            for d, (dc, dr, source, target, rows) in enumerate(ROUTES)
        ]

    def halo_rows(step):
        columns = []
        for c in range(6):
            tiles = [recv[step, pl.ds(80 * e + c, 16, stride=6), :] for e in range(4)]
            tiles += [recv[step, pl.ds(320 + c, 8, stride=8), :], jnp.zeros((8, 128), F32)]
            columns.append(jnp.concatenate(tiles, axis=0))
        return jnp.concatenate(columns, axis=1)

    def arrived(step):
        for copy, _, comes in exchange(step):
            pl.when(comes)(copy.wait_recv)
        return halo_rows(step)

    def one_step(step, carry):
        high, low = [dot(collect_ref[...], half).astype(BF16) * keep[...] for half in split(partial[...])]

        @pl.when(step == 0)
        def _():
            loads[4].wait()

        for c, value in enumerate(sample_blocks(*class_sums(high, low, inverse))):
            samples[c, :, :] = value

        @pl.when(step == 0)
        def _():
            loads[6].wait()

        @pl.when(step > 0)
        def _():
            rim = dot(table(3), jnp.concatenate(split(arrived(0)), axis=0))
            rim = jnp.where(natural < limit_col[0:EDGE_ROWS], -scales[STORED : STORED + EDGE_ROWS, 0:1] * rim, 0.0)
            for c, value in enumerate(sample_blocks(*class_sums(*split(rim), inverse))):
                for i in range(5):
                    for at, ends in (
                        (8 * i, ((i, picks[0]), (20 + i, picks[1]))),
                        (40 + 8 * i, ((5 * i, picks[2]), (5 * i + 4, picks[3]))),
                    ):
                        tile = value[at : at + 8, :]
                        for p, chosen in ends:
                            samples[c, 8 * p : 8 * p + 8, :] = samples[c, 8 * p : 8 * p + 8, :] + jnp.where(
                                chosen, tile, 0.0
                            )

        outer_forces(samples, mat, forces)
        value = coefficients([rim_tiles(forces, c, picks) for c in range(6)], forward)
        value = jnp.where(natural < limit_col[0:EDGE_ROWS], value, 0.0)
        edges = dot(table(6), jnp.concatenate(split(value), axis=0))
        sending = exchange(step)

        def pack(slots):
            for c in range(6):
                values = edges[:, 128 * c : 128 * c + 128]
                for e in slots:
                    send[step, pl.ds(80 * e + c, SIDE, stride=6), :] = values[16 * e : 16 * e + SIDE]

        def start(routes):
            for copy, goes, _ in routes:
                pl.when(goes)(copy.start)

        pack((3, 2))

        @pl.when(step == 0)
        def _():
            pl.semaphore_wait(barrier, expected)

        start(sending[0:2])
        for c in range(6):
            send[step, pl.ds(320 + c, 4, stride=8), :] = edges[64:68, 128 * c : 128 * c + 128]
        start(sending[2:6])
        pack((1, 0))
        start(sending[6:8])

        high, low = split(slabs_of(samples, MAIN, 32))
        slopes = dot(table(4), jnp.concatenate([high, high, low], axis=0))
        modulus = mat_centre[...]
        high, low = split(jnp.concatenate([slopes[:32] * modulus, slopes[32:] * modulus], axis=0))
        centre = dot(table(5), jnp.concatenate([high, high, low], axis=0))
        for c in range(6):
            forces[c, MAIN : MAIN + 32, :] = centre[:, 128 * c : 128 * c + 128]
        value = coefficients([forces[c, :, :] for c in range(6)], forward)
        coefs = jnp.concatenate(split(jnp.where(natural < limit_col, value, 0.0)), axis=0)

        @pl.when(step == 0)
        def _():
            for load in loads[7:]:
                load.wait()
            step_pad[0:1, 0:POINTS] = stepping[...]
            step_row = step_pad[0:1, :]
            diagonal = stored_row == lax.broadcasted_iota(jnp.int32, (STORED, STORED), 1)
            step_col = jnp.sum(jnp.where(diagonal, step_row, 0.0), axis=1, keepdims=True)
            scales[0:STORED, :] = jnp.broadcast_to(step_col, (STORED, 128))
            rim_step = jnp.sum(stored_of(table(2)) * step_row, axis=1, keepdims=True)
            scales[STORED:, :] = jnp.broadcast_to(rim_step, (EDGE_ROWS, 128))
            assemble[...] = dot(one_hot, gather[...]).astype(BF16)
            settle[...] = dot(one_hot, table(1)).astype(BF16)
            partial[...] = 2.0 * field[...] - by_class(padded(prev), lane)

        @pl.when(step > 0)
        def _():
            settled = dot(settle[...], jnp.concatenate(split(halo_rows(0)), axis=0))
            partial[...] = 2.0 * (partial[...] - scales[0:STORED, 0:1] * settled) - field[...]

        partial[...] = partial[...] - scales[0:STORED, 0:1] * dot(assemble[...], coefs)
        return carry

    lax.fori_loop(0, TIME_STEPS, one_step, 0)
    last = by_column(partial[...], lane)
    settled = dot(settle[...], jnp.concatenate(split(by_column(arrived(TIME_STEPS - 1), lane)), axis=0))
    out_ref[...] = (last - scales[0:STORED, 0:1] * settled)[0:POINTS]
    for step in range(TIME_STEPS):
        for copy, goes, _ in exchange(step):
            pl.when(goes)(copy.wait_send)


def solution(mesh):
    rows_total = mesh.shape["dom"] // GRID_COLUMNS
    inverse, forward = transform_tables()
    packed, gather = static_tables()

    def local(current, previous, material, stepping, point_order, order_bucket):
        operands = [
            current,
            point_order,
            packed,
            order_bucket,
            inverse,
            material,
            forward,
            stepping.reshape(1, POINTS),
            gather,
            previous,
        ]
        operands = [
            pltpu.with_memory_space_constraint(jnp.asarray(operand), pltpu.HBM) for operand in operands
        ]
        return pl.pallas_call(
            functools.partial(kernel, rows_total),
            out_shape=jax.ShapeDtypeStruct((POINTS, COLS), F32),
            in_specs=[pl.BlockSpec(memory_space=pltpu.HBM)] * len(operands),
            out_specs=pl.BlockSpec(memory_space=pltpu.VMEM),
            scratch_shapes=[pltpu.VMEM(operand.shape, operand.dtype) for operand in operands]
            + [
                pltpu.VMEM((8, STORED), jnp.int32),
                pltpu.VMEM((8, STORED), F32),
                pltpu.VMEM((6, MAIN, 128), F32),
                pltpu.VMEM((32, COLS), F32),
                pltpu.VMEM((6, ROWS, 128), F32),
                pltpu.VMEM((6, ROWS, 128), F32),
                pltpu.VMEM((ROWS, COLS), BF16),
                pltpu.VMEM((STORED, COLS), F32),
                pltpu.VMEM((STORED, COLS), F32),
                pltpu.VMEM((STORED + EDGE_ROWS, 128), F32),
                pltpu.VMEM((ROWS, STORED), BF16),
                pltpu.VMEM((STORED, 2 * ROWS), BF16),
                pltpu.VMEM((STORED, 2 * HALO), BF16),
                pltpu.VMEM((TIME_STEPS, MESSAGE_ROWS, 128), F32),
                pltpu.VMEM((TIME_STEPS, MESSAGE_ROWS, 128), F32),
                pltpu.SemaphoreType.DMA((len(operands),)),
                pltpu.SemaphoreType.DMA((TIME_STEPS, 8)),
                pltpu.SemaphoreType.DMA((TIME_STEPS, 8)),
            ],
            compiler_params=pltpu.CompilerParams(
                collective_id=0, has_side_effects=True, vmem_limit_bytes=VMEM_GRANT
            ),
        )(*operands)

    return jax.shard_map(
        local,
        mesh=mesh,
        in_specs=(
            P("dom", None),
            P("dom", None),
            P("dom", None, None),
            P("dom"),
            P("dom", None),
            P("dom", None),
        ),
        out_specs=P("dom", None),
        check_vma=False,
    )
```

```python
import functools

import jax
import jax.numpy as jnp
import ml_dtypes
import numpy as np
from jax import lax
from jax.experimental import pallas as pl
from jax.experimental.pallas import tpu as pltpu
from jax.sharding import PartitionSpec as P

ELEM_SIDE = 3
TIME_STEPS = 2
GRID_COLUMNS = 8
SIDE = 4 * ELEM_SIDE + 1
POINTS = SIDE * SIDE
COLS = 768
ELEMS = ELEM_SIDE * ELEM_SIDE
CENTRE = ELEMS // 2
MAIN = 200
ROWS = 240
STORED = 176
HALO = 80

VMEM_GRANT = 48 * 1024 * 1024

MESH = pl.DeviceIdType.MESH
BF16 = jnp.bfloat16
F32 = jnp.float32

MESSAGE_ROWS = 384
ROUTES = (
    (1, 1, 344, 320, 8),
    (-1, 1, 336, 328, 8),
    (1, -1, 328, 336, 8),
    (-1, -1, 320, 344, 8),
    (0, 1, 240, 160, 80),
    (0, -1, 160, 240, 80),
    (1, 0, 80, 0, 80),
    (-1, 0, 0, 80, 80),
)
EDGE_ROWS = 80


def split_np(table):
    high = table.astype(np.float32).astype(ml_dtypes.bfloat16)
    low = (table - high.astype(np.float64)).astype(np.float32).astype(ml_dtypes.bfloat16)
    return np.stack([high, low])


def gll_tables():
    nodes = np.array([-1.0, -np.sqrt(3.0 / 7.0), 0.0, np.sqrt(3.0 / 7.0), 1.0])
    weights = np.array([0.1, 49.0 / 90.0, 32.0 / 45.0, 49.0 / 90.0, 0.1])
    bary = np.array([1.0 / np.prod([nodes[j] - nodes[k] for k in range(5) if k != j]) for j in range(5)])
    derivative = np.zeros((5, 5))
    for i in range(5):
        for j in range(5):
            if i != j:
                derivative[i, j] = bary[j] / bary[i] / (nodes[i] - nodes[j])
        derivative[i, i] = -np.sum(derivative[i])
    return derivative, np.outer(weights, weights)


SHAPES = ((ROWS, STORED), (STORED, 2 * HALO), (EDGE_ROWS, STORED), (EDGE_ROWS, 2 * HALO), (64, 96), (32, 192), (HALO, 2 * EDGE_ROWS))
PACKED = tuple((sum(r for r, _ in SHAPES[:i]), rows, columns) for i, (rows, columns) in enumerate(SHAPES))
PACKED_ROWS = sum(r for r, _ in SHAPES)

DERIV, QUAD = gll_tables()
ODD = [[float(DERIV[i, j] - DERIV[i, 4 - j]) / 2 for j in range(2)] for i in range(2)]
EVEN = [[float(DERIV[i, j] + DERIV[i, 4 - j]) / 2 for j in range(2)] for i in range(2)]
MIDDLE = [float(DERIV[2, j]) for j in range(2)]
ODD_T = [[float(DERIV[c, a] - DERIV[4 - c, a]) / 2 for c in range(2)] for a in range(2)]
EVEN_T = [[float(DERIV[c, a] + DERIV[4 - c, a]) / 2 for c in range(2)] + [float(DERIV[2, a])] for a in range(2)]
MIDDLE_T = [float(DERIV[c, 2]) for c in range(2)]


BLOCKS = ((0, 0), (1, 0), (0, 1), (0, 2), (1, 1), (1, 2))


def block_columns(parity, kind):
    lane = np.arange(128)
    half = (lane % 4) // 2
    source = lane + 2 * (parity - half)
    return 128 * ((kind - (source // 2) % 3) % 3 + 3 * half) + source


def stacked(table):
    return np.concatenate(list(split_np(table)))


def squared(table):
    high, low = split_np(table)
    return np.concatenate([np.concatenate([high, low], axis=1), np.concatenate([high, 0 * low], axis=1)])


def transform_tables():
    sample = np.arange(128)

    def parts(parity, kind):
        column = block_columns(parity, kind)
        order = column // 2
        angle = (order[:, None] * sample[None, :] % COLS) * (2.0 * np.pi / COLS)
        even = (column % 2 == 0)[:, None]
        real = np.where(even, np.cos(angle), np.sin(angle))
        turned = np.where(even, -np.sin(angle), np.cos(angle)) * (np.sqrt(3.0) / 2.0)
        scale = np.where(order == 0, 1.0, 2.0) / COLS
        return real, turned, scale[:, None]

    tables = [[], [], [], []]
    for parity in range(2):
        real, _, scale = parts(parity, 0)
        tables[0].append(squared(real))
        tables[2].append(squared((real * scale).T))
        real1, turned1, scale1 = parts(parity, 1)
        real2, turned2, scale2 = parts(parity, 2)
        real, scale = np.concatenate([real1, real2]), np.concatenate([scale1, scale2])
        both = np.concatenate([real, np.concatenate([turned1, -turned2])], axis=1)
        tables[1].append(stacked(both))
        tables[3].append(stacked((both * scale).T))
    return np.concatenate(tables[0] + tables[1]), np.concatenate(tables[2] + tables[3])


def row_places():
    elem, point = np.full(ROWS, -1), np.full(ROWS, 0)
    outer = [e for e in range(ELEMS) if e != CENTRE]
    elem[:MAIN] = np.tile(outer, 25)
    point[:MAIN] = np.repeat(np.arange(25), 8)
    elem[MAIN : MAIN + 25] = CENTRE
    point[MAIN : MAIN + 25] = np.arange(25)
    return elem, point


def static_tables():
    elem, point = row_places()
    a, b = point // 5, point % 5
    used = elem >= 0
    struct = np.where(used, (4 * (elem // ELEM_SIDE) + a) * SIDE + 4 * (elem % ELEM_SIDE) + b, -1)
    gather = (np.arange(POINTS)[:, None] == struct[None, :]).astype(np.float64)
    gather = np.concatenate([gather, np.zeros((STORED - POINTS, ROWS))])
    place = np.zeros((STORED, HALO))
    along = np.arange(SIDE)
    edges = (along, 12 * SIDE + along, along * SIDE, along * SIDE + 12)
    corners = (0, 12 * SIDE, 12, 12 * SIDE + 12)
    for slot, (edge, corner) in enumerate(zip(edges, corners)):
        place[edge, 16 * slot + along] = 1.0
        place[corner, 64 + slot] = 1.0

    five = np.arange(25)
    fa, fb = five // 5, five % 5
    first = np.where(fb[:, None] == fb[None, :], DERIV[fa[:, None], fa[None, :]], 0.0)
    second = np.where(fa[:, None] == fa[None, :], DERIV[fb[:, None], fb[None, :]], 0.0)
    slope = np.zeros((64, 32))
    slope[:25, :25] = first
    slope[32:57, :25] = second
    weight = np.zeros(64)
    weight[:25] = weight[32:57] = QUAD[fa, fb]

    def across(table):
        high, low = split_np(table)
        return np.concatenate([high, low, high], axis=1)

    rim = np.full(EDGE_ROWS, -1)
    outer = [e for e in range(ELEMS) if e != CENTRE]
    for i in range(5):
        for q, e in enumerate(outer):
            ex, ey = e // ELEM_SIDE, e % ELEM_SIDE
            if ex != 1:
                rim[8 * i + q] = (4 * ex + 2 * ex) * SIDE + 4 * ey + i
            covered = (ex == 0 and i == 0) or (ex == 2 and i == 4)
            if ey != 1 and not covered:
                rim[40 + 8 * i + q] = (4 * ex + i) * SIDE + 6 * ey
    outgoing = np.zeros((HALO, EDGE_ROWS))
    for slot, (edge, corner) in enumerate(zip(edges, corners)):
        outgoing[16 * slot : 16 * slot + SIDE] = edge[:, None] == rim[None, :]
        outgoing[64 + slot] = corner == rim
    rim_gather = (rim[:, None] == np.arange(STORED)[None, :]).astype(np.float64)

    twice = lambda table: np.concatenate([table, table], axis=1)
    packed = np.zeros((PACKED_ROWS, 256), ml_dtypes.bfloat16)
    for (first, rows, columns), table in zip(
        PACKED,
        (
            gather.T,
            twice(place),
            rim_gather,
            twice(rim_gather @ place),
            across(slope),
            across(slope.T * weight[None, :]),
            twice(outgoing),
        ),
    ):
        packed[first : first + rows, :columns] = table.astype(ml_dtypes.bfloat16)
    return packed, twice(gather).astype(ml_dtypes.bfloat16)


def split(value):
    high = value.astype(BF16)
    return high, (value - high.astype(F32)).astype(BF16)


def dot(left, right):
    return jnp.dot(left, right, preferred_element_type=F32)


def slope_line(u):
    odd0, odd1, twice = u[0] - u[4], u[1] - u[3], u[2] + u[2]
    even0, even1 = u[0] + u[4] - twice, u[1] + u[3] - twice
    plus, minus = [], []
    for i in range(2):
        plus.append(ODD[i][0] * odd0 + ODD[i][1] * odd1)
        minus.append(EVEN[i][0] * even0 + EVEN[i][1] * even1)
    middle = MIDDLE[0] * odd0 + MIDDLE[1] * odd1
    return [plus[0] + minus[0], plus[1] + minus[1], middle, plus[1] - minus[1], plus[0] - minus[0]]


def force_line(s):
    odd0, odd1 = s[0] - s[4], s[1] - s[3]
    even0, even1 = s[0] + s[4], s[1] + s[3]
    plus, minus = [], []
    for a in range(2):
        plus.append(ODD_T[a][0] * odd0 + ODD_T[a][1] * odd1)
        minus.append(EVEN_T[a][0] * even0 + EVEN_T[a][1] * even1 + EVEN_T[a][2] * s[2])
    middle = MIDDLE_T[0] * odd0 + MIDDLE_T[1] * odd1
    return [plus[0] + minus[0], plus[1] + minus[1], middle, plus[1] - minus[1], plus[0] - minus[0]]


def by_class(value, lane):
    kind_of_lane, early = lax.rem(lane // 2, 3), lax.rem(lane, 4) < 2
    slabs = [value[:, 128 * v : 128 * v + 128] for v in range(6)]
    blocks = {}
    for kind in range(3):
        first, second = [
            jnp.where(
                kind_of_lane == 0,
                slabs[kind + 3 * h],
                jnp.where(kind_of_lane == 1, slabs[(kind - 1) % 3 + 3 * h], slabs[(kind - 2) % 3 + 3 * h]),
            )
            for h in range(2)
        ]
        blocks[0, kind] = jnp.where(early, first, pltpu.roll(second, 2, 1))
        blocks[1, kind] = jnp.where(early, pltpu.roll(first, 126, 1), second)
    return jnp.concatenate([blocks[block] for block in BLOCKS], axis=1)


def by_column(value, lane):
    kind_of_lane, early = lax.rem(lane // 2, 3), lax.rem(lane, 4) < 2
    blocks = {block: value[:, 128 * i : 128 * i + 128] for i, block in enumerate(BLOCKS)}
    halves = [[], []]
    for kind in range(3):
        even, odd = blocks[0, kind], blocks[1, kind]
        halves[0].append(jnp.where(early, even, pltpu.roll(odd, 2, 1)))
        halves[1].append(jnp.where(early, pltpu.roll(even, 126, 1), odd))
    slabs = []
    for v in range(6):
        parts = halves[v // 3]
        slabs.append(
            jnp.where(
                kind_of_lane == 0, parts[v % 3], jnp.where(kind_of_lane == 1, parts[(v + 1) % 3], parts[(v + 2) % 3])
            )
        )
    return jnp.concatenate(slabs, axis=1)


def class_sums(high, low, table):
    first, others = [], []
    for parity in range(2):
        lanes = slice(128 * parity, 128 * parity + 128)
        both = dot(
            jnp.concatenate([high[:, lanes], low[:, lanes]], axis=1), table[256 * parity : 256 * parity + 256, :]
        )
        first.append(both[:, 0:128] + both[:, 128:256])
    for parity in range(2):
        lanes = slice(256 + 256 * parity, 512 + 256 * parity)
        at = 512 + 512 * parity
        rows = high.shape[0]
        through = dot(jnp.concatenate([high[:, lanes], low[:, lanes]], axis=0), table[at : at + 256, :])
        others.append(through[:rows] + (through[rows:] + dot(high[:, lanes], table[at + 256 : at + 512, :])))
    return first, others


def sample_blocks(bases, boths):
    parities = []
    for base, both in zip(bases, boths):
        real, turned = both[:, 0:128], both[:, 128:256]
        half = base - 0.5 * real
        parities.append((base + real, half + turned, half - turned))
    out = [None] * 6
    for t in range(3):
        out[2 * t] = parities[0][t] + parities[1][t]
        out[(2 * t + 3) % 6] = parities[0][t] - parities[1][t]
    return out


def coefficients(forces, table):
    out0, out12 = [], []
    for sign in (1, -1):
        parts = []
        for t in range(3):
            one, other = forces[2 * t], forces[(2 * t + 3) % 6]
            parts.append(one + other if sign > 0 else one - other)
        pair = parts[1] + parts[2]
        out0.append(parts[0] + pair)
        out12 += [parts[0] - 0.5 * pair, parts[1] - parts[2]]
    first, others = class_sums(*split(jnp.concatenate(out0 + out12, axis=1)), table)
    return jnp.concatenate(first + others, axis=1)


def rim_tiles(forces, c, picks):
    tiles = []
    for low, high, step, span in ((picks[0], picks[1], 1, 20), (picks[2], picks[3], 5, 4)):
        for i in range(5):
            p = step * i
            one, other = forces[c, 8 * p : 8 * p + 8, :], forces[c, 8 * (p + span) : 8 * (p + span) + 8, :]
            tiles.append(jnp.where(low, one, jnp.where(high, other, 0.0)))
    return jnp.concatenate(tiles, axis=0)


def outer_forces(samples, modulus, forces):
    def one_block(c, carry):
        def tile(ref, p):
            return ref[c, 8 * p : 8 * p + 8, :]

        for second in range(2):
            for i in range(5):
                places = [5 * i + j if second else 5 * j + i for j in range(5)]
                slopes = slope_line([tile(samples, p) for p in places])
                parts = force_line([slope * tile(modulus, p) for slope, p in zip(slopes, places)])
                for p, part in zip(places, parts):
                    forces[c, 8 * p : 8 * p + 8, :] = tile(forces, p) + part if second else part
        return carry

    lax.fori_loop(0, 6, one_block, 0)


def padded(ref):
    first = lax.broadcasted_iota(jnp.int32, (8, COLS), 0) == 0
    return jnp.concatenate([ref[0:168, :], jnp.where(first, ref[168:169, :], 0.0)], axis=0)


def slabs_of(ref, first, count):
    return jnp.concatenate([ref[c, first : first + count, :] for c in range(6)], axis=1)


def kernel(rows_total, *refs):
    sources, out_ref, held, refs = refs[:10], refs[10], refs[11:21], refs[21:]
    (order_pad, step_pad, mat, mat_centre, samples, forces, keep, field, partial) = refs[:9]
    (scales, collect_ref, assemble, settle, send, recv, load_sem, send_sem, recv_sem) = refs[9:]
    cur, order, packed, bucket, inverse, mat_in, forward, stepping, gather, prev = held

    me = lax.axis_index("dom")
    column = lax.rem(me, GRID_COLUMNS)
    row = lax.div(me, GRID_COLUMNS)

    loads = [pltpu.make_async_copy(sources[i], held[i], load_sem.at[i]) for i in range(10)]
    for i in (1, 2, 0, 3, 5, 4):
        loads[i].start()

    recv[...] = jnp.zeros_like(recv)
    for e in range(4):
        send[:, 80 * e + 72 : 80 * e + 80, :] = jnp.zeros((TIME_STEPS, 8, 128), F32)
    send[:, 320:352, :] = jnp.zeros((TIME_STEPS, 32, 128), F32)

    def exists(dc, dr):
        c, r = column + dc, row + dr
        return (c >= 0) & (c < GRID_COLUMNS) & (r >= 0) & (r < rows_total)

    barrier = pltpu.get_barrier_semaphore()
    expected = jnp.int32(0)
    for dc, dr, _, _, _ in ROUTES:
        here = exists(dc, dr)
        expected = expected + here.astype(jnp.int32)

        @pl.when(here)
        def _():
            pl.semaphore_signal(barrier, inc=1, device_id=(me + dc + GRID_COLUMNS * dr,), device_id_type=MESH)

    order_pad[...] = jnp.full(order_pad.shape, -1, jnp.int32)
    step_pad[...] = jnp.zeros_like(step_pad)
    forces[:, MAIN + 32 : ROWS, :] = jnp.zeros((6, ROWS - MAIN - 32, 128), F32)
    mat_centre[...] = jnp.zeros_like(mat_centre)
    lane = lax.broadcasted_iota(jnp.int32, (1, 128), 1)
    q = lax.broadcasted_iota(jnp.int32, (8, 128), 0)
    picks = (q < 3, q >= 5, (q == 0) | (q == 3) | (q == 5), (q == 2) | (q == 4) | (q == 7))

    place_at = lax.broadcasted_iota(jnp.int32, (1, COLS), 1)
    block, inside = place_at >> 7, place_at & 127
    parity = ((block == 1) | (block >= 4)).astype(jnp.int32)
    kind = jnp.where(block < 2, 0, jnp.where((block == 2) | (block == 4), 1, 2))
    half = (inside >> 1) & 1
    source = inside + 2 * (parity - half)
    natural = (128 * (lax.rem(kind + 3 - lax.rem(source >> 1, 3), 3) + 3 * half) + source).astype(F32)

    def table(i):
        first, rows, columns = PACKED[i]
        return packed[first : first + rows, 0:columns]

    loads[1].wait()
    order_pad[0:1, 0:POINTS] = order[...]
    stored_row = lax.broadcasted_iota(jnp.int32, (STORED, STORED), 0)
    one_hot = jnp.where(stored_row == order_pad[0:1, :], 1.0, 0.0).astype(BF16)

    def stored_of(selection):
        return lax.dot_general(selection, one_hot, (((1,), (1,)), ((), ())), preferred_element_type=F32)

    loads[2].wait()
    collect = stored_of(table(0)).astype(BF16)

    loads[3].wait()
    limit_row = lax.shift_right_logical(jnp.full((1, ELEMS), COLS, jnp.int32), 3 - bucket[...]).astype(F32)
    elem_row = lax.broadcasted_iota(jnp.int32, (ROWS, ELEMS), 0)
    inner = lax.rem(elem_row, 8)
    owner = jnp.where(elem_row < MAIN, inner + (inner >= CENTRE).astype(jnp.int32), CENTRE)
    owned = owner == lax.broadcasted_iota(jnp.int32, (ROWS, ELEMS), 1)
    limit_col = jnp.sum(jnp.where(owned, limit_row, 0.0), axis=1, keepdims=True)
    keep[...] = jnp.where(natural < limit_col, 1.0, 0.0).astype(BF16)

    collect_ref[...] = collect
    loads[0].wait()
    field[...] = by_class(padded(cur), lane)
    partial[...] = field[...]
    for load in loads[6:]:
        load.start()
    loads[5].wait()
    for e in range(ELEMS):
        if e == CENTRE:
            mat_centre[0:25, :] = mat_in[e].astype(F32)
        else:
            for c in range(6):
                values = mat_in[e, :, 128 * c : 128 * c + 128].astype(F32)
                mat[c, pl.ds(e - (e > CENTRE), 25, stride=8), :] = values
    for p in range(25):
        mat[:, 8 * p : 8 * p + 8, :] = mat[:, 8 * p : 8 * p + 8, :] * float(QUAD[p // 5, p % 5])

    def exchange(step):
        return [
            (
                pltpu.make_async_remote_copy(
                    src_ref=send.at[step, pl.ds(source, rows)],
                    dst_ref=recv.at[step, pl.ds(target, rows)],
                    send_sem=send_sem.at[step, d],
                    recv_sem=recv_sem.at[step, d],
                    device_id=(me + dc + GRID_COLUMNS * dr,),
                    device_id_type=MESH,
                ),
                exists(dc, dr),
                exists(-dc, -dr),
            )
            for d, (dc, dr, source, target, rows) in enumerate(ROUTES)
        ]

    def halo_rows(step):
        columns = []
        for c in range(6):
            tiles = [recv[step, pl.ds(80 * e + c, 16, stride=6), :] for e in range(4)]
            tiles += [recv[step, pl.ds(320 + c, 8, stride=8), :], jnp.zeros((8, 128), F32)]
            columns.append(jnp.concatenate(tiles, axis=0))
        return jnp.concatenate(columns, axis=1)

    def arrived(step):
        for copy, _, comes in exchange(step):
            pl.when(comes)(copy.wait_recv)
        return halo_rows(step)

    def one_step(step, carry):
        high, low = [dot(collect_ref[...], half).astype(BF16) * keep[...] for half in split(partial[...])]

        @pl.when(step == 0)
        def _():
            loads[4].wait()

        for c, value in enumerate(sample_blocks(*class_sums(high, low, inverse))):
            samples[c, :, :] = value

        @pl.when(step == 0)
        def _():
            loads[6].wait()

        @pl.when(step > 0)
        def _():
            rim = dot(table(3), jnp.concatenate(split(arrived(0)), axis=0))
            rim = jnp.where(natural < limit_col[0:EDGE_ROWS], -scales[STORED : STORED + EDGE_ROWS, 0:1] * rim, 0.0)
            for c, value in enumerate(sample_blocks(*class_sums(*split(rim), inverse))):
                for i in range(5):
                    for at, ends in (
                        (8 * i, ((i, picks[0]), (20 + i, picks[1]))),
                        (40 + 8 * i, ((5 * i, picks[2]), (5 * i + 4, picks[3]))),
                    ):
                        tile = value[at : at + 8, :]
                        for p, chosen in ends:
                            samples[c, 8 * p : 8 * p + 8, :] = samples[c, 8 * p : 8 * p + 8, :] + jnp.where(
                                chosen, tile, 0.0
                            )

        outer_forces(samples, mat, forces)
        value = coefficients([rim_tiles(forces, c, picks) for c in range(6)], forward)
        value = jnp.where(natural < limit_col[0:EDGE_ROWS], value, 0.0)
        edges = dot(table(6), jnp.concatenate(split(value), axis=0))
        sending = exchange(step)

        def pack(slots):
            for c in range(6):
                values = edges[:, 128 * c : 128 * c + 128]
                for e in slots:
                    send[step, pl.ds(80 * e + c, SIDE, stride=6), :] = values[16 * e : 16 * e + SIDE]

        def start(routes):
            for copy, goes, _ in routes:
                pl.when(goes)(copy.start)

        for c in range(6):
            send[step, pl.ds(320 + c, 4, stride=8), :] = edges[64:68, 128 * c : 128 * c + 128]
        pack((3, 2))

        @pl.when(step == 0)
        def _():
            pl.semaphore_wait(barrier, expected)

        start(sending[0:6])
        pack((1, 0))
        start(sending[6:8])

        high, low = split(slabs_of(samples, MAIN, 32))
        slopes = dot(table(4), jnp.concatenate([high, high, low], axis=0))
        modulus = mat_centre[...]
        high, low = split(jnp.concatenate([slopes[:32] * modulus, slopes[32:] * modulus], axis=0))
        centre = dot(table(5), jnp.concatenate([high, high, low], axis=0))
        for c in range(6):
            forces[c, MAIN : MAIN + 32, :] = centre[:, 128 * c : 128 * c + 128]
        value = coefficients([forces[c, :, :] for c in range(6)], forward)
        coefs = jnp.concatenate(split(jnp.where(natural < limit_col, value, 0.0)), axis=0)

        @pl.when(step == 0)
        def _():
            for load in loads[7:]:
                load.wait()
            step_pad[0:1, 0:POINTS] = stepping[...]
            step_row = step_pad[0:1, :]
            diagonal = stored_row == lax.broadcasted_iota(jnp.int32, (STORED, STORED), 1)
            step_col = jnp.sum(jnp.where(diagonal, step_row, 0.0), axis=1, keepdims=True)
            scales[0:STORED, :] = jnp.broadcast_to(step_col, (STORED, 128))
            rim_step = jnp.sum(stored_of(table(2)) * step_row, axis=1, keepdims=True)
            scales[STORED:, :] = jnp.broadcast_to(rim_step, (EDGE_ROWS, 128))
            assemble[...] = dot(one_hot, gather[...]).astype(BF16)
            settle[...] = dot(one_hot, table(1)).astype(BF16)
            partial[...] = 2.0 * field[...] - by_class(padded(prev), lane)

        @pl.when(step > 0)
        def _():
            settled = dot(settle[...], jnp.concatenate(split(halo_rows(0)), axis=0))
            partial[...] = 2.0 * (partial[...] - scales[0:STORED, 0:1] * settled) - field[...]

        partial[...] = partial[...] - scales[0:STORED, 0:1] * dot(assemble[...], coefs)
        return carry

    lax.fori_loop(0, TIME_STEPS, one_step, 0)
    last = by_column(partial[...], lane)
    settled = dot(settle[...], jnp.concatenate(split(by_column(arrived(TIME_STEPS - 1), lane)), axis=0))
    out_ref[...] = (last - scales[0:STORED, 0:1] * settled)[0:POINTS]
    for step in range(TIME_STEPS):
        for copy, goes, _ in exchange(step):
            pl.when(goes)(copy.wait_send)


def solution(mesh):
    rows_total = mesh.shape["dom"] // GRID_COLUMNS
    inverse, forward = transform_tables()
    packed, gather = static_tables()

    def local(current, previous, material, stepping, point_order, order_bucket):
        operands = [
            current,
            point_order,
            packed,
            order_bucket,
            inverse,
            material,
            forward,
            stepping.reshape(1, POINTS),
            gather,
            previous,
        ]
        operands = [
            pltpu.with_memory_space_constraint(jnp.asarray(operand), pltpu.HBM) for operand in operands
        ]
        return pl.pallas_call(
            functools.partial(kernel, rows_total),
            out_shape=jax.ShapeDtypeStruct((POINTS, COLS), F32),
            in_specs=[pl.BlockSpec(memory_space=pltpu.HBM)] * len(operands),
            out_specs=pl.BlockSpec(memory_space=pltpu.VMEM),
            scratch_shapes=[pltpu.VMEM(operand.shape, operand.dtype) for operand in operands]
            + [
                pltpu.VMEM((8, STORED), jnp.int32),
                pltpu.VMEM((8, STORED), F32),
                pltpu.VMEM((6, MAIN, 128), F32),
                pltpu.VMEM((32, COLS), F32),
                pltpu.VMEM((6, ROWS, 128), F32),
                pltpu.VMEM((6, ROWS, 128), F32),
                pltpu.VMEM((ROWS, COLS), BF16),
                pltpu.VMEM((STORED, COLS), F32),
                pltpu.VMEM((STORED, COLS), F32),
                pltpu.VMEM((STORED + EDGE_ROWS, 128), F32),
                pltpu.VMEM((ROWS, STORED), BF16),
                pltpu.VMEM((STORED, 2 * ROWS), BF16),
                pltpu.VMEM((STORED, 2 * HALO), BF16),
                pltpu.VMEM((TIME_STEPS, MESSAGE_ROWS, 128), F32),
                pltpu.VMEM((TIME_STEPS, MESSAGE_ROWS, 128), F32),
                pltpu.SemaphoreType.DMA((len(operands),)),
                pltpu.SemaphoreType.DMA((TIME_STEPS, 8)),
                pltpu.SemaphoreType.DMA((TIME_STEPS, 8)),
            ],
            compiler_params=pltpu.CompilerParams(
                collective_id=0, has_side_effects=True, vmem_limit_bytes=VMEM_GRANT
            ),
        )(*operands)

    return jax.shard_map(
        local,
        mesh=mesh,
        in_specs=(
            P("dom", None),
            P("dom", None),
            P("dom", None, None),
            P("dom"),
            P("dom", None),
            P("dom", None),
        ),
        out_specs=P("dom", None),
        check_vma=False,
    )
```

```python
import functools

import jax
import jax.numpy as jnp
import ml_dtypes
import numpy as np
from jax import lax
from jax.experimental import pallas as pl
from jax.experimental.pallas import tpu as pltpu
from jax.sharding import PartitionSpec as P

ELEM_SIDE = 3
TIME_STEPS = 2
GRID_COLUMNS = 8
SIDE = 4 * ELEM_SIDE + 1
POINTS = SIDE * SIDE
COLS = 768
ELEMS = ELEM_SIDE * ELEM_SIDE
CENTRE = ELEMS // 2
MAIN = 200
ROWS = 240
STORED = 176
HALO = 80

VMEM_GRANT = 48 * 1024 * 1024

MESH = pl.DeviceIdType.MESH
BF16 = jnp.bfloat16
F32 = jnp.float32

MESSAGE_ROWS = 384
ROUTES = (
    (1, 1, 344, 320, 8),
    (-1, 1, 336, 328, 8),
    (1, -1, 328, 336, 8),
    (-1, -1, 320, 344, 8),
    (0, 1, 240, 160, 80),
    (0, -1, 160, 240, 80),
    (1, 0, 80, 0, 80),
    (-1, 0, 0, 80, 80),
)
EDGE_ROWS = 80


def split_np(table):
    high = table.astype(np.float32).astype(ml_dtypes.bfloat16)
    low = (table - high.astype(np.float64)).astype(np.float32).astype(ml_dtypes.bfloat16)
    return np.stack([high, low])


def gll_tables():
    nodes = np.array([-1.0, -np.sqrt(3.0 / 7.0), 0.0, np.sqrt(3.0 / 7.0), 1.0])
    weights = np.array([0.1, 49.0 / 90.0, 32.0 / 45.0, 49.0 / 90.0, 0.1])
    bary = np.array([1.0 / np.prod([nodes[j] - nodes[k] for k in range(5) if k != j]) for j in range(5)])
    derivative = np.zeros((5, 5))
    for i in range(5):
        for j in range(5):
            if i != j:
                derivative[i, j] = bary[j] / bary[i] / (nodes[i] - nodes[j])
        derivative[i, i] = -np.sum(derivative[i])
    return derivative, np.outer(weights, weights)


SHAPES = ((ROWS, STORED), (STORED, 2 * HALO), (EDGE_ROWS, STORED), (EDGE_ROWS, 2 * HALO), (64, 96), (32, 192), (HALO, 2 * EDGE_ROWS))
PACKED = tuple((sum(r for r, _ in SHAPES[:i]), rows, columns) for i, (rows, columns) in enumerate(SHAPES))
PACKED_ROWS = sum(r for r, _ in SHAPES)

DERIV, QUAD = gll_tables()
ODD = [[float(DERIV[i, j] - DERIV[i, 4 - j]) / 2 for j in range(2)] for i in range(2)]
EVEN = [[float(DERIV[i, j] + DERIV[i, 4 - j]) / 2 for j in range(2)] for i in range(2)]
MIDDLE = [float(DERIV[2, j]) for j in range(2)]
ODD_T = [[float(DERIV[c, a] - DERIV[4 - c, a]) / 2 for c in range(2)] for a in range(2)]
EVEN_T = [[float(DERIV[c, a] + DERIV[4 - c, a]) / 2 for c in range(2)] + [float(DERIV[2, a])] for a in range(2)]
MIDDLE_T = [float(DERIV[c, 2]) for c in range(2)]


BLOCKS = ((0, 0), (1, 0), (0, 1), (0, 2), (1, 1), (1, 2))


def block_columns(parity, kind):
    lane = np.arange(128)
    half = (lane % 4) // 2
    source = lane + 2 * (parity - half)
    return 128 * ((kind - (source // 2) % 3) % 3 + 3 * half) + source


def stacked(table):
    return np.concatenate(list(split_np(table)))


def squared(table):
    high, low = split_np(table)
    return np.concatenate([np.concatenate([high, low], axis=1), np.concatenate([high, 0 * low], axis=1)])


def transform_tables():
    sample = np.arange(128)

    def parts(parity, kind):
        column = block_columns(parity, kind)
        order = column // 2
        angle = (order[:, None] * sample[None, :] % COLS) * (2.0 * np.pi / COLS)
        even = (column % 2 == 0)[:, None]
        real = np.where(even, np.cos(angle), np.sin(angle))
        turned = np.where(even, -np.sin(angle), np.cos(angle)) * (np.sqrt(3.0) / 2.0)
        scale = np.where(order == 0, 1.0, 2.0) / COLS
        return real, turned, scale[:, None]

    tables = [[], [], [], []]
    for parity in range(2):
        real, _, scale = parts(parity, 0)
        tables[0].append(squared(real))
        tables[2].append(squared((real * scale).T))
        real1, turned1, scale1 = parts(parity, 1)
        real2, turned2, scale2 = parts(parity, 2)
        real, scale = np.concatenate([real1, real2]), np.concatenate([scale1, scale2])
        both = np.concatenate([real, np.concatenate([turned1, -turned2])], axis=1)
        tables[1].append(stacked(both))
        tables[3].append(stacked((both * scale).T))
    return np.concatenate(tables[0] + tables[1]), np.concatenate(tables[2] + tables[3])


def row_places():
    elem, point = np.full(ROWS, -1), np.full(ROWS, 0)
    outer = [e for e in range(ELEMS) if e != CENTRE]
    elem[:MAIN] = np.tile(outer, 25)
    point[:MAIN] = np.repeat(np.arange(25), 8)
    elem[MAIN : MAIN + 25] = CENTRE
    point[MAIN : MAIN + 25] = np.arange(25)
    return elem, point


def static_tables():
    elem, point = row_places()
    a, b = point // 5, point % 5
    used = elem >= 0
    struct = np.where(used, (4 * (elem // ELEM_SIDE) + a) * SIDE + 4 * (elem % ELEM_SIDE) + b, -1)
    gather = (np.arange(POINTS)[:, None] == struct[None, :]).astype(np.float64)
    gather = np.concatenate([gather, np.zeros((STORED - POINTS, ROWS))])
    place = np.zeros((STORED, HALO))
    along = np.arange(SIDE)
    edges = (along, 12 * SIDE + along, along * SIDE, along * SIDE + 12)
    corners = (0, 12 * SIDE, 12, 12 * SIDE + 12)
    for slot, (edge, corner) in enumerate(zip(edges, corners)):
        place[edge, 16 * slot + along] = 1.0
        place[corner, 64 + slot] = 1.0

    five = np.arange(25)
    fa, fb = five // 5, five % 5
    first = np.where(fb[:, None] == fb[None, :], DERIV[fa[:, None], fa[None, :]], 0.0)
    second = np.where(fa[:, None] == fa[None, :], DERIV[fb[:, None], fb[None, :]], 0.0)
    slope = np.zeros((64, 32))
    slope[:25, :25] = first
    slope[32:57, :25] = second
    weight = np.zeros(64)
    weight[:25] = weight[32:57] = QUAD[fa, fb]

    def across(table):
        high, low = split_np(table)
        return np.concatenate([high, low, high], axis=1)

    rim = np.full(EDGE_ROWS, -1)
    outer = [e for e in range(ELEMS) if e != CENTRE]
    for i in range(5):
        for q, e in enumerate(outer):
            ex, ey = e // ELEM_SIDE, e % ELEM_SIDE
            if ex != 1:
                rim[8 * i + q] = (4 * ex + 2 * ex) * SIDE + 4 * ey + i
            covered = (ex == 0 and i == 0) or (ex == 2 and i == 4)
            if ey != 1 and not covered:
                rim[40 + 8 * i + q] = (4 * ex + i) * SIDE + 6 * ey
    outgoing = np.zeros((HALO, EDGE_ROWS))
    for slot, (edge, corner) in enumerate(zip(edges, corners)):
        outgoing[16 * slot : 16 * slot + SIDE] = edge[:, None] == rim[None, :]
        outgoing[64 + slot] = corner == rim
    rim_gather = (rim[:, None] == np.arange(STORED)[None, :]).astype(np.float64)

    twice = lambda table: np.concatenate([table, table], axis=1)
    packed = np.zeros((PACKED_ROWS, 256), ml_dtypes.bfloat16)
    for (first, rows, columns), table in zip(
        PACKED,
        (
            gather.T,
            twice(place),
            rim_gather,
            twice(rim_gather @ place),
            across(slope),
            across(slope.T * weight[None, :]),
            twice(outgoing),
        ),
    ):
        packed[first : first + rows, :columns] = table.astype(ml_dtypes.bfloat16)
    return packed, twice(gather).astype(ml_dtypes.bfloat16)


def split(value):
    high = value.astype(BF16)
    return high, (value - high.astype(F32)).astype(BF16)


def dot(left, right):
    return jnp.dot(left, right, preferred_element_type=F32)


def slope_line(u):
    odd0, odd1, twice = u[0] - u[4], u[1] - u[3], u[2] + u[2]
    even0, even1 = u[0] + u[4] - twice, u[1] + u[3] - twice
    plus, minus = [], []
    for i in range(2):
        plus.append(ODD[i][0] * odd0 + ODD[i][1] * odd1)
        minus.append(EVEN[i][0] * even0 + EVEN[i][1] * even1)
    middle = MIDDLE[0] * odd0 + MIDDLE[1] * odd1
    return [plus[0] + minus[0], plus[1] + minus[1], middle, plus[1] - minus[1], plus[0] - minus[0]]


def force_line(s):
    odd0, odd1 = s[0] - s[4], s[1] - s[3]
    even0, even1 = s[0] + s[4], s[1] + s[3]
    plus, minus = [], []
    for a in range(2):
        plus.append(ODD_T[a][0] * odd0 + ODD_T[a][1] * odd1)
        minus.append(EVEN_T[a][0] * even0 + EVEN_T[a][1] * even1 + EVEN_T[a][2] * s[2])
    middle = MIDDLE_T[0] * odd0 + MIDDLE_T[1] * odd1
    return [plus[0] + minus[0], plus[1] + minus[1], middle, plus[1] - minus[1], plus[0] - minus[0]]


def by_class(value, lane):
    kind_of_lane, early = lax.rem(lane // 2, 3), lax.rem(lane, 4) < 2
    slabs = [value[:, 128 * v : 128 * v + 128] for v in range(6)]
    blocks = {}
    for kind in range(3):
        first, second = [
            jnp.where(
                kind_of_lane == 0,
                slabs[kind + 3 * h],
                jnp.where(kind_of_lane == 1, slabs[(kind - 1) % 3 + 3 * h], slabs[(kind - 2) % 3 + 3 * h]),
            )
            for h in range(2)
        ]
        blocks[0, kind] = jnp.where(early, first, pltpu.roll(second, 2, 1))
        blocks[1, kind] = jnp.where(early, pltpu.roll(first, 126, 1), second)
    return jnp.concatenate([blocks[block] for block in BLOCKS], axis=1)


def by_column(value, lane):
    kind_of_lane, early = lax.rem(lane // 2, 3), lax.rem(lane, 4) < 2
    blocks = {block: value[:, 128 * i : 128 * i + 128] for i, block in enumerate(BLOCKS)}
    halves = [[], []]
    for kind in range(3):
        even, odd = blocks[0, kind], blocks[1, kind]
        halves[0].append(jnp.where(early, even, pltpu.roll(odd, 2, 1)))
        halves[1].append(jnp.where(early, pltpu.roll(even, 126, 1), odd))
    slabs = []
    for v in range(6):
        parts = halves[v // 3]
        slabs.append(
            jnp.where(
                kind_of_lane == 0, parts[v % 3], jnp.where(kind_of_lane == 1, parts[(v + 1) % 3], parts[(v + 2) % 3])
            )
        )
    return jnp.concatenate(slabs, axis=1)


def class_sums(high, low, table):
    first, others = [], []
    for parity in range(2):
        lanes = slice(128 * parity, 128 * parity + 128)
        both = dot(
            jnp.concatenate([high[:, lanes], low[:, lanes]], axis=1), table[256 * parity : 256 * parity + 256, :]
        )
        first.append(both[:, 0:128] + both[:, 128:256])
    for parity in range(2):
        lanes = slice(256 + 256 * parity, 512 + 256 * parity)
        at = 512 + 512 * parity
        rows = high.shape[0]
        through = dot(jnp.concatenate([high[:, lanes], low[:, lanes]], axis=0), table[at : at + 256, :])
        others.append(through[:rows] + (through[rows:] + dot(high[:, lanes], table[at + 256 : at + 512, :])))
    return first, others


def sample_blocks(bases, boths):
    parities = []
    for base, both in zip(bases, boths):
        real, turned = both[:, 0:128], both[:, 128:256]
        half = base - 0.5 * real
        parities.append((base + real, half + turned, half - turned))
    out = [None] * 6
    for t in range(3):
        out[2 * t] = parities[0][t] + parities[1][t]
        out[(2 * t + 3) % 6] = parities[0][t] - parities[1][t]
    return out


def coefficients(forces, table):
    out0, out12 = [], []
    for sign in (1, -1):
        parts = []
        for t in range(3):
            one, other = forces[2 * t], forces[(2 * t + 3) % 6]
            parts.append(one + other if sign > 0 else one - other)
        pair = parts[1] + parts[2]
        out0.append(parts[0] + pair)
        out12 += [parts[0] - 0.5 * pair, parts[1] - parts[2]]
    first, others = class_sums(*split(jnp.concatenate(out0 + out12, axis=1)), table)
    return jnp.concatenate(first + others, axis=1)


def rim_tiles(forces, c, picks):
    tiles = []
    for low, high, step, span in ((picks[0], picks[1], 1, 20), (picks[2], picks[3], 5, 4)):
        for i in range(5):
            p = step * i
            one, other = forces[c, 8 * p : 8 * p + 8, :], forces[c, 8 * (p + span) : 8 * (p + span) + 8, :]
            tiles.append(jnp.where(low, one, jnp.where(high, other, 0.0)))
    return jnp.concatenate(tiles, axis=0)


def outer_forces(samples, modulus, forces):
    def one_block(c, carry):
        def tile(ref, p):
            return ref[c, 8 * p : 8 * p + 8, :]

        for second in range(2):
            for i in range(5):
                places = [5 * i + j if second else 5 * j + i for j in range(5)]
                slopes = slope_line([tile(samples, p) for p in places])
                parts = force_line([slope * tile(modulus, p) for slope, p in zip(slopes, places)])
                for p, part in zip(places, parts):
                    forces[c, 8 * p : 8 * p + 8, :] = tile(forces, p) + part if second else part
        return carry

    lax.fori_loop(0, 6, one_block, 0)


def padded(ref):
    first = lax.broadcasted_iota(jnp.int32, (8, COLS), 0) == 0
    return jnp.concatenate([ref[0:168, :], jnp.where(first, ref[168:169, :], 0.0)], axis=0)


def slabs_of(ref, first, count):
    return jnp.concatenate([ref[c, first : first + count, :] for c in range(6)], axis=1)


def kernel(rows_total, *refs):
    sources, out_ref, held, refs = refs[:10], refs[10], refs[11:21], refs[21:]
    (order_pad, step_pad, mat, mat_centre, samples, forces, keep, field, partial) = refs[:9]
    (scales, collect_ref, assemble, settle, send, recv, load_sem, send_sem, recv_sem) = refs[9:]
    cur, order, packed, bucket, inverse, mat_in, forward, stepping, gather, prev = held

    me = lax.axis_index("dom")
    column = lax.rem(me, GRID_COLUMNS)
    row = lax.div(me, GRID_COLUMNS)

    loads = [pltpu.make_async_copy(sources[i], held[i], load_sem.at[i]) for i in range(10)]
    for i in (1, 2, 0, 3, 5, 4):
        loads[i].start()

    recv[...] = jnp.zeros_like(recv)
    for e in range(4):
        send[:, 80 * e + 72 : 80 * e + 80, :] = jnp.zeros((TIME_STEPS, 8, 128), F32)
    send[:, 320:352, :] = jnp.zeros((TIME_STEPS, 32, 128), F32)

    def exists(dc, dr):
        c, r = column + dc, row + dr
        return (c >= 0) & (c < GRID_COLUMNS) & (r >= 0) & (r < rows_total)

    barrier = pltpu.get_barrier_semaphore()
    expected = jnp.int32(0)
    for dc, dr, _, _, _ in ROUTES:
        here = exists(dc, dr)
        expected = expected + here.astype(jnp.int32)

        @pl.when(here)
        def _():
            pl.semaphore_signal(barrier, inc=1, device_id=(me + dc + GRID_COLUMNS * dr,), device_id_type=MESH)

    order_pad[...] = jnp.full(order_pad.shape, -1, jnp.int32)
    step_pad[...] = jnp.zeros_like(step_pad)
    forces[:, MAIN + 32 : ROWS, :] = jnp.zeros((6, ROWS - MAIN - 32, 128), F32)
    mat_centre[...] = jnp.zeros_like(mat_centre)
    lane = lax.broadcasted_iota(jnp.int32, (1, 128), 1)
    q = lax.broadcasted_iota(jnp.int32, (8, 128), 0)
    picks = (q < 3, q >= 5, (q == 0) | (q == 3) | (q == 5), (q == 2) | (q == 4) | (q == 7))

    place_at = lax.broadcasted_iota(jnp.int32, (1, COLS), 1)
    block, inside = place_at >> 7, place_at & 127
    parity = ((block == 1) | (block >= 4)).astype(jnp.int32)
    kind = jnp.where(block < 2, 0, jnp.where((block == 2) | (block == 4), 1, 2))
    half = (inside >> 1) & 1
    source = inside + 2 * (parity - half)
    natural = (128 * (lax.rem(kind + 3 - lax.rem(source >> 1, 3), 3) + 3 * half) + source).astype(F32)

    def table(i):
        first, rows, columns = PACKED[i]
        return packed[first : first + rows, 0:columns]

    loads[1].wait()
    order_pad[0:1, 0:POINTS] = order[...]
    stored_row = lax.broadcasted_iota(jnp.int32, (STORED, STORED), 0)
    one_hot = jnp.where(stored_row == order_pad[0:1, :], 1.0, 0.0).astype(BF16)

    def stored_of(selection):
        return lax.dot_general(selection, one_hot, (((1,), (1,)), ((), ())), preferred_element_type=F32)

    loads[2].wait()
    collect = stored_of(table(0)).astype(BF16)

    loads[3].wait()
    limit_row = lax.shift_right_logical(jnp.full((1, ELEMS), COLS, jnp.int32), 3 - bucket[...]).astype(F32)
    elem_row = lax.broadcasted_iota(jnp.int32, (ROWS, ELEMS), 0)
    inner = lax.rem(elem_row, 8)
    owner = jnp.where(elem_row < MAIN, inner + (inner >= CENTRE).astype(jnp.int32), CENTRE)
    owned = owner == lax.broadcasted_iota(jnp.int32, (ROWS, ELEMS), 1)
    limit_col = jnp.sum(jnp.where(owned, limit_row, 0.0), axis=1, keepdims=True)
    keep[...] = jnp.where(natural < limit_col, 1.0, 0.0).astype(BF16)

    collect_ref[...] = collect
    loads[0].wait()
    field[...] = by_class(padded(cur), lane)
    partial[...] = field[...]
    for load in loads[6:]:
        load.start()
    loads[5].wait()
    for e in range(ELEMS):
        if e == CENTRE:
            mat_centre[0:25, :] = mat_in[e].astype(F32)
        else:
            for c in range(6):
                values = mat_in[e, :, 128 * c : 128 * c + 128].astype(F32)
                mat[c, pl.ds(e - (e > CENTRE), 25, stride=8), :] = values
    for p in range(25):
        mat[:, 8 * p : 8 * p + 8, :] = mat[:, 8 * p : 8 * p + 8, :] * float(QUAD[p // 5, p % 5])

    def exchange(step):
        return [
            (
                pltpu.make_async_remote_copy(
                    src_ref=send.at[step, pl.ds(source, rows)],
                    dst_ref=recv.at[step, pl.ds(target, rows)],
                    send_sem=send_sem.at[step, d],
                    recv_sem=recv_sem.at[step, d],
                    device_id=(me + dc + GRID_COLUMNS * dr,),
                    device_id_type=MESH,
                ),
                exists(dc, dr),
                exists(-dc, -dr),
            )
            for d, (dc, dr, source, target, rows) in enumerate(ROUTES)
        ]

    def halo_rows(step):
        columns = []
        for c in range(6):
            tiles = [recv[step, pl.ds(80 * e + c, 16, stride=6), :] for e in range(4)]
            tiles += [recv[step, pl.ds(320 + c, 8, stride=8), :], jnp.zeros((8, 128), F32)]
            columns.append(jnp.concatenate(tiles, axis=0))
        return jnp.concatenate(columns, axis=1)

    def arrived(step):
        for copy, _, comes in exchange(step):
            pl.when(comes)(copy.wait_recv)
        return halo_rows(step)

    def one_step(step, carry):
        high, low = [dot(collect_ref[...], half).astype(BF16) * keep[...] for half in split(partial[...])]

        @pl.when(step == 0)
        def _():
            loads[4].wait()

        for c, value in enumerate(sample_blocks(*class_sums(high, low, inverse))):
            samples[c, :, :] = value

        @pl.when(step == 0)
        def _():
            loads[6].wait()

        @pl.when(step > 0)
        def _():
            rim = dot(table(3), jnp.concatenate(split(arrived(0)), axis=0))
            rim = jnp.where(natural < limit_col[0:EDGE_ROWS], -scales[STORED : STORED + EDGE_ROWS, 0:1] * rim, 0.0)
            for c, value in enumerate(sample_blocks(*class_sums(*split(rim), inverse))):
                for i in range(5):
                    for at, ends in (
                        (8 * i, ((i, picks[0]), (20 + i, picks[1]))),
                        (40 + 8 * i, ((5 * i, picks[2]), (5 * i + 4, picks[3]))),
                    ):
                        tile = value[at : at + 8, :]
                        for p, chosen in ends:
                            samples[c, 8 * p : 8 * p + 8, :] = samples[c, 8 * p : 8 * p + 8, :] + jnp.where(
                                chosen, tile, 0.0
                            )

        outer_forces(samples, mat, forces)
        value = coefficients([rim_tiles(forces, c, picks) for c in range(6)], forward)
        value = jnp.where(natural < limit_col[0:EDGE_ROWS], value, 0.0)
        edges = dot(table(6), jnp.concatenate(split(value), axis=0))
        sending = exchange(step)

        def pack(slots):
            for c in range(6):
                values = edges[:, 128 * c : 128 * c + 128]
                for e in slots:
                    send[step, pl.ds(80 * e + c, SIDE, stride=6), :] = values[16 * e : 16 * e + SIDE]

        def start(routes):
            for copy, goes, _ in routes:
                pl.when(goes)(copy.start)

        for c in range(6):
            send[step, pl.ds(320 + c, 4, stride=8), :] = edges[64:68, 128 * c : 128 * c + 128]
        pack((3, 2))

        @pl.when(step == 0)
        def _():
            pl.semaphore_wait(barrier, expected)

        even = lax.rem(me, 2) == 0
        for copy, goes, _ in sending[4:6]:
            pl.when(goes & even)(copy.start)
        start(sending[0:4])
        for copy, goes, _ in sending[4:6]:
            pl.when(goes & jnp.logical_not(even))(copy.start)
        pack((1, 0))
        start(sending[6:8])

        high, low = split(slabs_of(samples, MAIN, 32))
        slopes = dot(table(4), jnp.concatenate([high, high, low], axis=0))
        modulus = mat_centre[...]
        high, low = split(jnp.concatenate([slopes[:32] * modulus, slopes[32:] * modulus], axis=0))
        centre = dot(table(5), jnp.concatenate([high, high, low], axis=0))
        for c in range(6):
            forces[c, MAIN : MAIN + 32, :] = centre[:, 128 * c : 128 * c + 128]
        value = coefficients([forces[c, :, :] for c in range(6)], forward)
        coefs = jnp.concatenate(split(jnp.where(natural < limit_col, value, 0.0)), axis=0)

        @pl.when(step == 0)
        def _():
            for load in loads[7:]:
                load.wait()
            step_pad[0:1, 0:POINTS] = stepping[...]
            step_row = step_pad[0:1, :]
            diagonal = stored_row == lax.broadcasted_iota(jnp.int32, (STORED, STORED), 1)
            step_col = jnp.sum(jnp.where(diagonal, step_row, 0.0), axis=1, keepdims=True)
            scales[0:STORED, :] = jnp.broadcast_to(step_col, (STORED, 128))
            rim_step = jnp.sum(stored_of(table(2)) * step_row, axis=1, keepdims=True)
            scales[STORED:, :] = jnp.broadcast_to(rim_step, (EDGE_ROWS, 128))
            assemble[...] = dot(one_hot, gather[...]).astype(BF16)
            settle[...] = dot(one_hot, table(1)).astype(BF16)
            partial[...] = 2.0 * field[...] - by_class(padded(prev), lane)

        @pl.when(step > 0)
        def _():
            settled = dot(settle[...], jnp.concatenate(split(halo_rows(0)), axis=0))
            partial[...] = 2.0 * (partial[...] - scales[0:STORED, 0:1] * settled) - field[...]

        partial[...] = partial[...] - scales[0:STORED, 0:1] * dot(assemble[...], coefs)
        return carry

    lax.fori_loop(0, TIME_STEPS, one_step, 0)
    last = by_column(partial[...], lane)
    settled = dot(settle[...], jnp.concatenate(split(by_column(arrived(TIME_STEPS - 1), lane)), axis=0))
    out_ref[...] = (last - scales[0:STORED, 0:1] * settled)[0:POINTS]
    for step in range(TIME_STEPS):
        for copy, goes, _ in exchange(step):
            pl.when(goes)(copy.wait_send)


def solution(mesh):
    rows_total = mesh.shape["dom"] // GRID_COLUMNS
    inverse, forward = transform_tables()
    packed, gather = static_tables()

    def local(current, previous, material, stepping, point_order, order_bucket):
        operands = [
            current,
            point_order,
            packed,
            order_bucket,
            inverse,
            material,
            forward,
            stepping.reshape(1, POINTS),
            gather,
            previous,
        ]
        operands = [
            pltpu.with_memory_space_constraint(jnp.asarray(operand), pltpu.HBM) for operand in operands
        ]
        return pl.pallas_call(
            functools.partial(kernel, rows_total),
            out_shape=jax.ShapeDtypeStruct((POINTS, COLS), F32),
            in_specs=[pl.BlockSpec(memory_space=pltpu.HBM)] * len(operands),
            out_specs=pl.BlockSpec(memory_space=pltpu.VMEM),
            scratch_shapes=[pltpu.VMEM(operand.shape, operand.dtype) for operand in operands]
            + [
                pltpu.VMEM((8, STORED), jnp.int32),
                pltpu.VMEM((8, STORED), F32),
                pltpu.VMEM((6, MAIN, 128), F32),
                pltpu.VMEM((32, COLS), F32),
                pltpu.VMEM((6, ROWS, 128), F32),
                pltpu.VMEM((6, ROWS, 128), F32),
                pltpu.VMEM((ROWS, COLS), BF16),
                pltpu.VMEM((STORED, COLS), F32),
                pltpu.VMEM((STORED, COLS), F32),
                pltpu.VMEM((STORED + EDGE_ROWS, 128), F32),
                pltpu.VMEM((ROWS, STORED), BF16),
                pltpu.VMEM((STORED, 2 * ROWS), BF16),
                pltpu.VMEM((STORED, 2 * HALO), BF16),
                pltpu.VMEM((TIME_STEPS, MESSAGE_ROWS, 128), F32),
                pltpu.VMEM((TIME_STEPS, MESSAGE_ROWS, 128), F32),
                pltpu.SemaphoreType.DMA((len(operands),)),
                pltpu.SemaphoreType.DMA((TIME_STEPS, 8)),
                pltpu.SemaphoreType.DMA((TIME_STEPS, 8)),
            ],
            compiler_params=pltpu.CompilerParams(
                collective_id=0, has_side_effects=True, vmem_limit_bytes=VMEM_GRANT
            ),
        )(*operands)

    return jax.shard_map(
        local,
        mesh=mesh,
        in_specs=(
            P("dom", None),
            P("dom", None),
            P("dom", None, None),
            P("dom"),
            P("dom", None),
            P("dom", None),
        ),
        out_specs=P("dom", None),
        check_vma=False,
    )
```

```python
import functools

import jax
import jax.numpy as jnp
import ml_dtypes
import numpy as np
from jax import lax
from jax.experimental import pallas as pl
from jax.experimental.pallas import tpu as pltpu
from jax.sharding import PartitionSpec as P

ELEM_SIDE = 3
TIME_STEPS = 2
GRID_COLUMNS = 8
SIDE = 4 * ELEM_SIDE + 1
POINTS = SIDE * SIDE
COLS = 768
ELEMS = ELEM_SIDE * ELEM_SIDE
CENTRE = ELEMS // 2
MAIN = 200
ROWS = 240
STORED = 176
HALO = 80

VMEM_GRANT = 48 * 1024 * 1024

MESH = pl.DeviceIdType.MESH
BF16 = jnp.bfloat16
F32 = jnp.float32

MESSAGE_ROWS = 384
ROUTES = (
    (1, 1, 344, 320, 8),
    (-1, 1, 336, 328, 8),
    (1, -1, 328, 336, 8),
    (-1, -1, 320, 344, 8),
    (0, 1, 240, 160, 80),
    (0, -1, 160, 240, 80),
    (1, 0, 80, 0, 80),
    (-1, 0, 0, 80, 80),
)
EDGE_ROWS = 80


def split_np(table):
    high = table.astype(np.float32).astype(ml_dtypes.bfloat16)
    low = (table - high.astype(np.float64)).astype(np.float32).astype(ml_dtypes.bfloat16)
    return np.stack([high, low])


def gll_tables():
    nodes = np.array([-1.0, -np.sqrt(3.0 / 7.0), 0.0, np.sqrt(3.0 / 7.0), 1.0])
    weights = np.array([0.1, 49.0 / 90.0, 32.0 / 45.0, 49.0 / 90.0, 0.1])
    bary = np.array([1.0 / np.prod([nodes[j] - nodes[k] for k in range(5) if k != j]) for j in range(5)])
    derivative = np.zeros((5, 5))
    for i in range(5):
        for j in range(5):
            if i != j:
                derivative[i, j] = bary[j] / bary[i] / (nodes[i] - nodes[j])
        derivative[i, i] = -np.sum(derivative[i])
    return derivative, np.outer(weights, weights)


SHAPES = ((ROWS, STORED), (STORED, 2 * HALO), (EDGE_ROWS, STORED), (EDGE_ROWS, 2 * HALO), (64, 96), (32, 192), (HALO, 2 * EDGE_ROWS))
PACKED = tuple((sum(r for r, _ in SHAPES[:i]), rows, columns) for i, (rows, columns) in enumerate(SHAPES))
PACKED_ROWS = sum(r for r, _ in SHAPES)

DERIV, QUAD = gll_tables()
ODD = [[float(DERIV[i, j] - DERIV[i, 4 - j]) / 2 for j in range(2)] for i in range(2)]
EVEN = [[float(DERIV[i, j] + DERIV[i, 4 - j]) / 2 for j in range(2)] for i in range(2)]
MIDDLE = [float(DERIV[2, j]) for j in range(2)]
ODD_T = [[float(DERIV[c, a] - DERIV[4 - c, a]) / 2 for c in range(2)] for a in range(2)]
EVEN_T = [[float(DERIV[c, a] + DERIV[4 - c, a]) / 2 for c in range(2)] + [float(DERIV[2, a])] for a in range(2)]
MIDDLE_T = [float(DERIV[c, 2]) for c in range(2)]


BLOCKS = ((0, 0), (1, 0), (0, 1), (0, 2), (1, 1), (1, 2))


def block_columns(parity, kind):
    lane = np.arange(128)
    half = (lane % 4) // 2
    source = lane + 2 * (parity - half)
    return 128 * ((kind - (source // 2) % 3) % 3 + 3 * half) + source


def stacked(table):
    return np.concatenate(list(split_np(table)))


def squared(table):
    high, low = split_np(table)
    return np.concatenate([np.concatenate([high, low], axis=1), np.concatenate([high, 0 * low], axis=1)])


def transform_tables():
    sample = np.arange(128)

    def parts(parity, kind):
        column = block_columns(parity, kind)
        order = column // 2
        angle = (order[:, None] * sample[None, :] % COLS) * (2.0 * np.pi / COLS)
        even = (column % 2 == 0)[:, None]
        real = np.where(even, np.cos(angle), np.sin(angle))
        turned = np.where(even, -np.sin(angle), np.cos(angle)) * (np.sqrt(3.0) / 2.0)
        scale = np.where(order == 0, 1.0, 2.0) / COLS
        return real, turned, scale[:, None]

    tables = [[], [], [], []]
    for parity in range(2):
        real, _, scale = parts(parity, 0)
        tables[0].append(squared(real))
        tables[2].append(squared((real * scale).T))
        real1, turned1, scale1 = parts(parity, 1)
        real2, turned2, scale2 = parts(parity, 2)
        real, scale = np.concatenate([real1, real2]), np.concatenate([scale1, scale2])
        both = np.concatenate([real, np.concatenate([turned1, -turned2])], axis=1)
        tables[1].append(stacked(both))
        tables[3].append(stacked((both * scale).T))
    return np.concatenate(tables[0] + tables[1]), np.concatenate(tables[2] + tables[3])


def row_places():
    elem, point = np.full(ROWS, -1), np.full(ROWS, 0)
    outer = [e for e in range(ELEMS) if e != CENTRE]
    elem[:MAIN] = np.tile(outer, 25)
    point[:MAIN] = np.repeat(np.arange(25), 8)
    elem[MAIN : MAIN + 25] = CENTRE
    point[MAIN : MAIN + 25] = np.arange(25)
    return elem, point


def static_tables():
    elem, point = row_places()
    a, b = point // 5, point % 5
    used = elem >= 0
    struct = np.where(used, (4 * (elem // ELEM_SIDE) + a) * SIDE + 4 * (elem % ELEM_SIDE) + b, -1)
    gather = (np.arange(POINTS)[:, None] == struct[None, :]).astype(np.float64)
    gather = np.concatenate([gather, np.zeros((STORED - POINTS, ROWS))])
    place = np.zeros((STORED, HALO))
    along = np.arange(SIDE)
    edges = (along, 12 * SIDE + along, along * SIDE, along * SIDE + 12)
    corners = (0, 12 * SIDE, 12, 12 * SIDE + 12)
    for slot, (edge, corner) in enumerate(zip(edges, corners)):
        place[edge, 16 * slot + along] = 1.0
        place[corner, 64 + slot] = 1.0

    five = np.arange(25)
    fa, fb = five // 5, five % 5
    first = np.where(fb[:, None] == fb[None, :], DERIV[fa[:, None], fa[None, :]], 0.0)
    second = np.where(fa[:, None] == fa[None, :], DERIV[fb[:, None], fb[None, :]], 0.0)
    slope = np.zeros((64, 32))
    slope[:25, :25] = first
    slope[32:57, :25] = second
    weight = np.zeros(64)
    weight[:25] = weight[32:57] = QUAD[fa, fb]

    def across(table):
        high, low = split_np(table)
        return np.concatenate([high, low, high], axis=1)

    rim = np.full(EDGE_ROWS, -1)
    outer = [e for e in range(ELEMS) if e != CENTRE]
    for i in range(5):
        for q, e in enumerate(outer):
            ex, ey = e // ELEM_SIDE, e % ELEM_SIDE
            if ex != 1:
                rim[8 * i + q] = (4 * ex + 2 * ex) * SIDE + 4 * ey + i
            covered = (ex == 0 and i == 0) or (ex == 2 and i == 4)
            if ey != 1 and not covered:
                rim[40 + 8 * i + q] = (4 * ex + i) * SIDE + 6 * ey
    outgoing = np.zeros((HALO, EDGE_ROWS))
    for slot, (edge, corner) in enumerate(zip(edges, corners)):
        outgoing[16 * slot : 16 * slot + SIDE] = edge[:, None] == rim[None, :]
        outgoing[64 + slot] = corner == rim
    rim_gather = (rim[:, None] == np.arange(STORED)[None, :]).astype(np.float64)

    twice = lambda table: np.concatenate([table, table], axis=1)
    packed = np.zeros((PACKED_ROWS, 256), ml_dtypes.bfloat16)
    for (first, rows, columns), table in zip(
        PACKED,
        (
            gather.T,
            twice(place),
            rim_gather,
            twice(rim_gather @ place),
            across(slope),
            across(slope.T * weight[None, :]),
            twice(outgoing),
        ),
    ):
        packed[first : first + rows, :columns] = table.astype(ml_dtypes.bfloat16)
    return packed, twice(gather).astype(ml_dtypes.bfloat16)


def split(value):
    high = value.astype(BF16)
    return high, (value - high.astype(F32)).astype(BF16)


def dot(left, right):
    return jnp.dot(left, right, preferred_element_type=F32)


def slope_line(u):
    odd0, odd1, twice = u[0] - u[4], u[1] - u[3], u[2] + u[2]
    even0, even1 = u[0] + u[4] - twice, u[1] + u[3] - twice
    plus, minus = [], []
    for i in range(2):
        plus.append(ODD[i][0] * odd0 + ODD[i][1] * odd1)
        minus.append(EVEN[i][0] * even0 + EVEN[i][1] * even1)
    middle = MIDDLE[0] * odd0 + MIDDLE[1] * odd1
    return [plus[0] + minus[0], plus[1] + minus[1], middle, plus[1] - minus[1], plus[0] - minus[0]]


def force_line(s):
    odd0, odd1 = s[0] - s[4], s[1] - s[3]
    even0, even1 = s[0] + s[4], s[1] + s[3]
    plus, minus = [], []
    for a in range(2):
        plus.append(ODD_T[a][0] * odd0 + ODD_T[a][1] * odd1)
        minus.append(EVEN_T[a][0] * even0 + EVEN_T[a][1] * even1 + EVEN_T[a][2] * s[2])
    middle = MIDDLE_T[0] * odd0 + MIDDLE_T[1] * odd1
    return [plus[0] + minus[0], plus[1] + minus[1], middle, plus[1] - minus[1], plus[0] - minus[0]]


def by_class(value, lane):
    kind_of_lane, early = lax.rem(lane // 2, 3), lax.rem(lane, 4) < 2
    slabs = [value[:, 128 * v : 128 * v + 128] for v in range(6)]
    blocks = {}
    for kind in range(3):
        first, second = [
            jnp.where(
                kind_of_lane == 0,
                slabs[kind + 3 * h],
                jnp.where(kind_of_lane == 1, slabs[(kind - 1) % 3 + 3 * h], slabs[(kind - 2) % 3 + 3 * h]),
            )
            for h in range(2)
        ]
        blocks[0, kind] = jnp.where(early, first, pltpu.roll(second, 2, 1))
        blocks[1, kind] = jnp.where(early, pltpu.roll(first, 126, 1), second)
    return jnp.concatenate([blocks[block] for block in BLOCKS], axis=1)


def by_column(value, lane):
    kind_of_lane, early = lax.rem(lane // 2, 3), lax.rem(lane, 4) < 2
    blocks = {block: value[:, 128 * i : 128 * i + 128] for i, block in enumerate(BLOCKS)}
    halves = [[], []]
    for kind in range(3):
        even, odd = blocks[0, kind], blocks[1, kind]
        halves[0].append(jnp.where(early, even, pltpu.roll(odd, 2, 1)))
        halves[1].append(jnp.where(early, pltpu.roll(even, 126, 1), odd))
    slabs = []
    for v in range(6):
        parts = halves[v // 3]
        slabs.append(
            jnp.where(
                kind_of_lane == 0, parts[v % 3], jnp.where(kind_of_lane == 1, parts[(v + 1) % 3], parts[(v + 2) % 3])
            )
        )
    return jnp.concatenate(slabs, axis=1)


def class_sums(high, low, table):
    first, others = [], []
    for parity in range(2):
        lanes = slice(128 * parity, 128 * parity + 128)
        both = dot(
            jnp.concatenate([high[:, lanes], low[:, lanes]], axis=1), table[256 * parity : 256 * parity + 256, :]
        )
        first.append(both[:, 0:128] + both[:, 128:256])
    for parity in range(2):
        lanes = slice(256 + 256 * parity, 512 + 256 * parity)
        at = 512 + 512 * parity
        rows = high.shape[0]
        through = dot(jnp.concatenate([high[:, lanes], low[:, lanes]], axis=0), table[at : at + 256, :])
        others.append(through[:rows] + (through[rows:] + dot(high[:, lanes], table[at + 256 : at + 512, :])))
    return first, others


def sample_blocks(bases, boths):
    parities = []
    for base, both in zip(bases, boths):
        real, turned = both[:, 0:128], both[:, 128:256]
        half = base - 0.5 * real
        parities.append((base + real, half + turned, half - turned))
    out = [None] * 6
    for t in range(3):
        out[2 * t] = parities[0][t] + parities[1][t]
        out[(2 * t + 3) % 6] = parities[0][t] - parities[1][t]
    return out


def coefficients(forces, table):
    out0, out12 = [], []
    for sign in (1, -1):
        parts = []
        for t in range(3):
            one, other = forces[2 * t], forces[(2 * t + 3) % 6]
            parts.append(one + other if sign > 0 else one - other)
        pair = parts[1] + parts[2]
        out0.append(parts[0] + pair)
        out12 += [parts[0] - 0.5 * pair, parts[1] - parts[2]]
    first, others = class_sums(*split(jnp.concatenate(out0 + out12, axis=1)), table)
    return jnp.concatenate(first + others, axis=1)


def rim_tiles(forces, c, picks):
    tiles = []
    for low, high, step, span in ((picks[0], picks[1], 1, 20), (picks[2], picks[3], 5, 4)):
        for i in range(5):
            p = step * i
            one, other = forces[c, 8 * p : 8 * p + 8, :], forces[c, 8 * (p + span) : 8 * (p + span) + 8, :]
            tiles.append(jnp.where(low, one, jnp.where(high, other, 0.0)))
    return jnp.concatenate(tiles, axis=0)


def outer_forces(samples, modulus, forces):
    def one_block(c, carry):
        def tile(ref, p):
            return ref[c, 8 * p : 8 * p + 8, :]

        for second in range(2):
            for i in range(5):
                places = [5 * i + j if second else 5 * j + i for j in range(5)]
                slopes = slope_line([tile(samples, p) for p in places])
                parts = force_line([slope * tile(modulus, p) for slope, p in zip(slopes, places)])
                for p, part in zip(places, parts):
                    forces[c, 8 * p : 8 * p + 8, :] = tile(forces, p) + part if second else part
        return carry

    lax.fori_loop(0, 6, one_block, 0, unroll=2)


def padded(ref):
    first = lax.broadcasted_iota(jnp.int32, (8, COLS), 0) == 0
    return jnp.concatenate([ref[0:168, :], jnp.where(first, ref[168:169, :], 0.0)], axis=0)


def slabs_of(ref, first, count):
    return jnp.concatenate([ref[c, first : first + count, :] for c in range(6)], axis=1)


def kernel(rows_total, *refs):
    sources, out_ref, held, refs = refs[:10], refs[10], refs[11:21], refs[21:]
    (order_pad, step_pad, mat, mat_centre, samples, forces, keep, field, partial) = refs[:9]
    (scales, collect_ref, assemble, settle, send, recv, load_sem, send_sem, recv_sem) = refs[9:]
    cur, order, packed, bucket, inverse, mat_in, forward, stepping, gather, prev = held

    me = lax.axis_index("dom")
    column = lax.rem(me, GRID_COLUMNS)
    row = lax.div(me, GRID_COLUMNS)

    loads = [pltpu.make_async_copy(sources[i], held[i], load_sem.at[i]) for i in range(10)]
    for i in (1, 2, 0, 3, 5, 4):
        loads[i].start()

    recv[...] = jnp.zeros_like(recv)
    for e in range(4):
        send[:, 80 * e + 72 : 80 * e + 80, :] = jnp.zeros((TIME_STEPS, 8, 128), F32)
    send[:, 320:352, :] = jnp.zeros((TIME_STEPS, 32, 128), F32)

    def exists(dc, dr):
        c, r = column + dc, row + dr
        return (c >= 0) & (c < GRID_COLUMNS) & (r >= 0) & (r < rows_total)

    barrier = pltpu.get_barrier_semaphore()
    expected = jnp.int32(0)
    for dc, dr, _, _, _ in ROUTES:
        here = exists(dc, dr)
        expected = expected + here.astype(jnp.int32)

        @pl.when(here)
        def _():
            pl.semaphore_signal(barrier, inc=1, device_id=(me + dc + GRID_COLUMNS * dr,), device_id_type=MESH)

    order_pad[...] = jnp.full(order_pad.shape, -1, jnp.int32)
    step_pad[...] = jnp.zeros_like(step_pad)
    forces[:, MAIN + 32 : ROWS, :] = jnp.zeros((6, ROWS - MAIN - 32, 128), F32)
    mat_centre[...] = jnp.zeros_like(mat_centre)
    lane = lax.broadcasted_iota(jnp.int32, (1, 128), 1)
    q = lax.broadcasted_iota(jnp.int32, (8, 128), 0)
    picks = (q < 3, q >= 5, (q == 0) | (q == 3) | (q == 5), (q == 2) | (q == 4) | (q == 7))

    place_at = lax.broadcasted_iota(jnp.int32, (1, COLS), 1)
    block, inside = place_at >> 7, place_at & 127
    parity = ((block == 1) | (block >= 4)).astype(jnp.int32)
    kind = jnp.where(block < 2, 0, jnp.where((block == 2) | (block == 4), 1, 2))
    half = (inside >> 1) & 1
    source = inside + 2 * (parity - half)
    natural = (128 * (lax.rem(kind + 3 - lax.rem(source >> 1, 3), 3) + 3 * half) + source).astype(F32)

    def table(i):
        first, rows, columns = PACKED[i]
        return packed[first : first + rows, 0:columns]

    loads[1].wait()
    order_pad[0:1, 0:POINTS] = order[...]
    stored_row = lax.broadcasted_iota(jnp.int32, (STORED, STORED), 0)
    one_hot = jnp.where(stored_row == order_pad[0:1, :], 1.0, 0.0).astype(BF16)

    def stored_of(selection):
        return lax.dot_general(selection, one_hot, (((1,), (1,)), ((), ())), preferred_element_type=F32)

    loads[2].wait()
    collect = stored_of(table(0)).astype(BF16)

    loads[3].wait()
    limit_row = lax.shift_right_logical(jnp.full((1, ELEMS), COLS, jnp.int32), 3 - bucket[...]).astype(F32)
    elem_row = lax.broadcasted_iota(jnp.int32, (ROWS, ELEMS), 0)
    inner = lax.rem(elem_row, 8)
    owner = jnp.where(elem_row < MAIN, inner + (inner >= CENTRE).astype(jnp.int32), CENTRE)
    owned = owner == lax.broadcasted_iota(jnp.int32, (ROWS, ELEMS), 1)
    limit_col = jnp.sum(jnp.where(owned, limit_row, 0.0), axis=1, keepdims=True)
    keep[...] = jnp.where(natural < limit_col, 1.0, 0.0).astype(BF16)

    collect_ref[...] = collect
    loads[0].wait()
    field[...] = by_class(padded(cur), lane)
    partial[...] = field[...]
    for load in loads[6:]:
        load.start()
    loads[5].wait()
    for e in range(ELEMS):
        if e == CENTRE:
            mat_centre[0:25, :] = mat_in[e].astype(F32)
        else:
            for c in range(6):
                values = mat_in[e, :, 128 * c : 128 * c + 128].astype(F32)
                mat[c, pl.ds(e - (e > CENTRE), 25, stride=8), :] = values
    for p in range(25):
        mat[:, 8 * p : 8 * p + 8, :] = mat[:, 8 * p : 8 * p + 8, :] * float(QUAD[p // 5, p % 5])

    def exchange(step):
        return [
            (
                pltpu.make_async_remote_copy(
                    src_ref=send.at[step, pl.ds(source, rows)],
                    dst_ref=recv.at[step, pl.ds(target, rows)],
                    send_sem=send_sem.at[step, d],
                    recv_sem=recv_sem.at[step, d],
                    device_id=(me + dc + GRID_COLUMNS * dr,),
                    device_id_type=MESH,
                ),
                exists(dc, dr),
                exists(-dc, -dr),
            )
            for d, (dc, dr, source, target, rows) in enumerate(ROUTES)
        ]

    def halo_rows(step):
        columns = []
        for c in range(6):
            tiles = [recv[step, pl.ds(80 * e + c, 16, stride=6), :] for e in range(4)]
            tiles += [recv[step, pl.ds(320 + c, 8, stride=8), :], jnp.zeros((8, 128), F32)]
            columns.append(jnp.concatenate(tiles, axis=0))
        return jnp.concatenate(columns, axis=1)

    def arrived(step):
        for copy, _, comes in exchange(step):
            pl.when(comes)(copy.wait_recv)
        return halo_rows(step)

    def one_step(step, carry):
        high, low = [dot(collect_ref[...], half).astype(BF16) * keep[...] for half in split(partial[...])]

        @pl.when(step == 0)
        def _():
            loads[4].wait()

        for c, value in enumerate(sample_blocks(*class_sums(high, low, inverse))):
            samples[c, :, :] = value

        @pl.when(step == 0)
        def _():
            loads[6].wait()

        @pl.when(step > 0)
        def _():
            rim = dot(table(3), jnp.concatenate(split(arrived(0)), axis=0))
            rim = jnp.where(natural < limit_col[0:EDGE_ROWS], -scales[STORED : STORED + EDGE_ROWS, 0:1] * rim, 0.0)
            for c, value in enumerate(sample_blocks(*class_sums(*split(rim), inverse))):
                for i in range(5):
                    for at, ends in (
                        (8 * i, ((i, picks[0]), (20 + i, picks[1]))),
                        (40 + 8 * i, ((5 * i, picks[2]), (5 * i + 4, picks[3]))),
                    ):
                        tile = value[at : at + 8, :]
                        for p, chosen in ends:
                            samples[c, 8 * p : 8 * p + 8, :] = samples[c, 8 * p : 8 * p + 8, :] + jnp.where(
                                chosen, tile, 0.0
                            )

        outer_forces(samples, mat, forces)
        value = coefficients([rim_tiles(forces, c, picks) for c in range(6)], forward)
        value = jnp.where(natural < limit_col[0:EDGE_ROWS], value, 0.0)
        edges = dot(table(6), jnp.concatenate(split(value), axis=0))
        sending = exchange(step)

        def pack(slots):
            for c in range(6):
                values = edges[:, 128 * c : 128 * c + 128]
                for e in slots:
                    send[step, pl.ds(80 * e + c, SIDE, stride=6), :] = values[16 * e : 16 * e + SIDE]

        def start(routes):
            for copy, goes, _ in routes:
                pl.when(goes)(copy.start)

        for c in range(6):
            send[step, pl.ds(320 + c, 4, stride=8), :] = edges[64:68, 128 * c : 128 * c + 128]
        pack((3, 2))

        @pl.when(step == 0)
        def _():
            pl.semaphore_wait(barrier, expected)

        even = lax.rem(me, 2) == 0
        for copy, goes, _ in sending[4:6]:
            pl.when(goes & even)(copy.start)
        start(sending[0:4])
        for copy, goes, _ in sending[4:6]:
            pl.when(goes & jnp.logical_not(even))(copy.start)
        pack((1, 0))
        start(sending[6:8])

        high, low = split(slabs_of(samples, MAIN, 32))
        slopes = dot(table(4), jnp.concatenate([high, high, low], axis=0))
        modulus = mat_centre[...]
        high, low = split(jnp.concatenate([slopes[:32] * modulus, slopes[32:] * modulus], axis=0))
        centre = dot(table(5), jnp.concatenate([high, high, low], axis=0))
        for c in range(6):
            forces[c, MAIN : MAIN + 32, :] = centre[:, 128 * c : 128 * c + 128]
        value = coefficients([forces[c, :, :] for c in range(6)], forward)
        coefs = jnp.concatenate(split(jnp.where(natural < limit_col, value, 0.0)), axis=0)

        @pl.when(step == 0)
        def _():
            for load in loads[7:]:
                load.wait()
            step_pad[0:1, 0:POINTS] = stepping[...]
            step_row = step_pad[0:1, :]
            diagonal = stored_row == lax.broadcasted_iota(jnp.int32, (STORED, STORED), 1)
            step_col = jnp.sum(jnp.where(diagonal, step_row, 0.0), axis=1, keepdims=True)
            scales[0:STORED, :] = jnp.broadcast_to(step_col, (STORED, 128))
            rim_step = jnp.sum(stored_of(table(2)) * step_row, axis=1, keepdims=True)
            scales[STORED:, :] = jnp.broadcast_to(rim_step, (EDGE_ROWS, 128))
            assemble[...] = dot(one_hot, gather[...]).astype(BF16)
            settle[...] = dot(one_hot, table(1)).astype(BF16)
            partial[...] = 2.0 * field[...] - by_class(padded(prev), lane)

        @pl.when(step > 0)
        def _():
            settled = dot(settle[...], jnp.concatenate(split(halo_rows(0)), axis=0))
            partial[...] = 2.0 * (partial[...] - scales[0:STORED, 0:1] * settled) - field[...]

        partial[...] = partial[...] - scales[0:STORED, 0:1] * dot(assemble[...], coefs)
        return carry

    lax.fori_loop(0, TIME_STEPS, one_step, 0)
    last = by_column(partial[...], lane)
    settled = dot(settle[...], jnp.concatenate(split(by_column(arrived(TIME_STEPS - 1), lane)), axis=0))
    out_ref[...] = (last - scales[0:STORED, 0:1] * settled)[0:POINTS]
    for step in range(TIME_STEPS):
        for copy, goes, _ in exchange(step):
            pl.when(goes)(copy.wait_send)


def solution(mesh):
    rows_total = mesh.shape["dom"] // GRID_COLUMNS
    inverse, forward = transform_tables()
    packed, gather = static_tables()

    def local(current, previous, material, stepping, point_order, order_bucket):
        operands = [
            current,
            point_order,
            packed,
            order_bucket,
            inverse,
            material,
            forward,
            stepping.reshape(1, POINTS),
            gather,
            previous,
        ]
        operands = [
            pltpu.with_memory_space_constraint(jnp.asarray(operand), pltpu.HBM) for operand in operands
        ]
        return pl.pallas_call(
            functools.partial(kernel, rows_total),
            out_shape=jax.ShapeDtypeStruct((POINTS, COLS), F32),
            in_specs=[pl.BlockSpec(memory_space=pltpu.HBM)] * len(operands),
            out_specs=pl.BlockSpec(memory_space=pltpu.VMEM),
            scratch_shapes=[pltpu.VMEM(operand.shape, operand.dtype) for operand in operands]
            + [
                pltpu.VMEM((8, STORED), jnp.int32),
                pltpu.VMEM((8, STORED), F32),
                pltpu.VMEM((6, MAIN, 128), F32),
                pltpu.VMEM((32, COLS), F32),
                pltpu.VMEM((6, ROWS, 128), F32),
                pltpu.VMEM((6, ROWS, 128), F32),
                pltpu.VMEM((ROWS, COLS), BF16),
                pltpu.VMEM((STORED, COLS), F32),
                pltpu.VMEM((STORED, COLS), F32),
                pltpu.VMEM((STORED + EDGE_ROWS, 128), F32),
                pltpu.VMEM((ROWS, STORED), BF16),
                pltpu.VMEM((STORED, 2 * ROWS), BF16),
                pltpu.VMEM((STORED, 2 * HALO), BF16),
                pltpu.VMEM((TIME_STEPS, MESSAGE_ROWS, 128), F32),
                pltpu.VMEM((TIME_STEPS, MESSAGE_ROWS, 128), F32),
                pltpu.SemaphoreType.DMA((len(operands),)),
                pltpu.SemaphoreType.DMA((TIME_STEPS, 8)),
                pltpu.SemaphoreType.DMA((TIME_STEPS, 8)),
            ],
            compiler_params=pltpu.CompilerParams(
                collective_id=0, has_side_effects=True, vmem_limit_bytes=VMEM_GRANT
            ),
        )(*operands)

    return jax.shard_map(
        local,
        mesh=mesh,
        in_specs=(
            P("dom", None),
            P("dom", None),
            P("dom", None, None),
            P("dom"),
            P("dom", None),
            P("dom", None),
        ),
        out_specs=P("dom", None),
        check_vma=False,
    )
```
